128 devices in a mesh: rows: 32 (over x, y, core), cols: 4 (over z).
Axes of the slice: x: 4, y: 4, z: 4, core: 2. Of those that a mesh axis runs over, the one named last changes fastest.
Arguments:
- blocks: bfloat16 [16384, 128, 128], P(('rows', 'cols')), may hold values from -20 to 20
- owner: int32 [16384, 1], P(('rows', 'cols')), may hold values from 0 to 127; in each aligned block of 128 rows (0 to 127, 128 to 255, ...) at most 2 rows name the same one
- block_pos: int32 [16384], P(('rows', 'cols')), may hold values from 0 to 415
- omega: bfloat16 [53248, 512], P('cols'), may hold values from -0.02734375 to 0.02734375
Outputs:
- basis: bfloat16 [16384, 512], P('rows', 'cols')
- coefficients: float32 [512, 53248], P('rows', 'cols')
The draws below stay inside these ranges and needn't reach their ends.
Inputs may be any that keep to these rules, and one draw needn't show every extreme that they name: `owner`: among the slots of one device no tile is named more than 2 times, and on at least one device some tile is named exactly 2 times. `block_pos`: several slots may name the same block of the same tile; their blocks add.
All inputs are finite; a program needn't handle non-finite values.
Results may differ from the reference program's by a relative error of at most 0.0038.
Values may be sent and summed in bfloat16 or wider, within the bound.
No kernel may reach another device: no remote copies, remote signals or barrier semaphores. Data moves between devices by JAX's collectives and lax.ppermute only.
A program may use at most 192 MiB of HBM per device.

```python
import math
import jax
import jax.numpy as jnp
import numpy as np
from jax import lax

BLK = 128
RANK = 512
PBR = 4
TBC = 104
SLOT_DEV = 128
CAP = 2
SLOTS = 16384
PANEL = 512
TCOL = 13312
TBLK = 416
M = 16384
N = 53248
N_ROWS = 32
N_COLS = 4
DEVICES = 128


def draw_blocks(key, part):
    first, second, third = jax.random.split(key, 3)
    values = jnp.clip(jax.random.normal(first, (SLOTS, BLK, BLK), jnp.float32), -6.0, 6.0)
    row_scale = jnp.exp(jax.random.uniform(second, (SLOTS, BLK, 1), jnp.float32) * math.log(10.0)) / 10.0
    column_scale = jnp.exp(jax.random.uniform(third, (SLOTS, 1, BLK), jnp.float32) * math.log(3.0))
    return (values * row_scale * column_scale).astype(jnp.bfloat16)


def set_ends(result, key, least, high):
    longest = result.shape.index(max(result.shape))
    spots = []
    for shift in (0, 1):
        where = [jax.random.randint(jax.random.fold_in(key, axis), (), 0, length) for axis, length in enumerate(result.shape)]
        where[longest] = (where[longest] + shift) % result.shape[longest]
        spots.append(tuple(where))
    return result.at[spots[0]].set(least).at[spots[1]].set(high)


def block_scale(rng, shape, cuts, least, largest):
    def one(position, shards_of):
        draws = jax.random.uniform(jax.random.fold_in(jax.random.fold_in(rng, 6), position), (shards_of,), jnp.float32, least / len(cuts), largest / len(cuts))
        return jnp.repeat(jnp.exp(draws), shape[position] // shards_of).reshape((-1,) + (1,) * (len(shape) - position - 1))

    factor_of = one(*cuts[0])
    for cut in cuts[1:]:
        factor_of = factor_of * one(*cut)
    return factor_of


def assign_block(rng, own, number, rows, count, top, most, slope):
    ranking = jax.random.permutation(rng, count)
    crowded, ordinary = load_shares(count, rows * top, most, slope, True), load_shares(count, rows * top, most, slope, False)
    places = jnp.arange(count)

    def named(lengths, offset_by):
        used = int((lengths > 0).sum())
        fixed = max(1, used // 4)
        shifted = fixed + (places - fixed + offset_by * (used - fixed)) % max(1, count - fixed)
        return jnp.zeros((count,), jnp.int32).at[ranking[jnp.where(places < fixed, places, shifted)]].set(jnp.asarray(lengths, jnp.int32))

    lengths = jnp.where(number % 4 == 0, named(crowded, number // 4), named(ordinary, number - number // 4 - 1))
    mixed = jax.random.permutation(jax.random.fold_in(own, 3), count)
    giver, receiver = mixed[0:count // 2 * 2:2], mixed[1:count // 2 * 2:2]
    room = jnp.minimum(lengths[giver] - 1, most - lengths[receiver]) // 2
    room = jnp.where((giver == ranking[0]) | (receiver == ranking[0]) | (lengths[receiver] == 0), 0, jnp.maximum(room, 0))
    shifted = jax.random.randint(jax.random.fold_in(own, 4), (count // 2,), 0, 1 << 20) % (room + 1)
    lengths = lengths.at[giver].add(-shifted).at[receiver].add(shifted)
    items = jnp.searchsorted(jnp.cumsum(lengths), jnp.arange(rows * top), side="right").astype(jnp.int32)
    listing = items.reshape(top, rows).T
    listing = listing[jax.random.permutation(jax.random.fold_in(own, 1), rows)]
    offset_by = jax.random.randint(jax.random.fold_in(own, 2), (rows, 1), 0, top)
    return jnp.take_along_axis(listing, (jnp.arange(top)[None, :] + offset_by) % top, axis=1)


def load_shares(number_of, total, limit, skew, full):
    weights = [(1 << 20) // math.isqrt(standing ** skew) + 1 for standing in range(1, number_of + 1)]
    largest = limit if full else min(limit, max(-(-total // number_of), total * weights[0] // sum(weights)))
    least = 1 if total - largest >= number_of - 1 else 0
    given, spare = [largest] + [least] * (number_of - 1), total - largest - least * (number_of - 1)
    while spare > 0:
        candidates = [i for i in range(1, number_of) if given[i] < largest] or [i for i in range(1, number_of) if given[i] < limit]
        pool, remaining = sum([weights[i] for i in candidates]), spare
        for i in candidates:
            extra = min(limit - given[i], max(1, remaining * weights[i] // pool), spare)
            given[i] = given[i] + extra
            spare = spare - extra
    return np.array(given)


def normal_values(stream_key, shape, spread, limit, cuts=(), kind=jnp.bfloat16):
    values = jax.random.normal(stream_key, shape, jnp.float32) * spread
    if len(cuts) > 0:
        values = block_scale(stream_key, shape, cuts, -0.22, 0.18) * values
    return jnp.clip(values, min=-limit, max=limit).astype(kind)


def setup_inputs(seed: int = 0) -> dict:
    splits = jax.random.split(jax.random.key(seed), 5)
    blocks = draw_blocks(jax.random.fold_in(splits[4], 71), 0)
    owner_keys = jax.random.split(jax.random.fold_in(splits[1], 1), SLOTS // SLOT_DEV)
    owner_turns = jax.random.permutation(jax.random.fold_in(splits[1], 3), SLOTS // SLOT_DEV)
    owner = jax.vmap(lambda own, number: assign_block(jax.random.fold_in(splits[1], 2), own, number, SLOT_DEV, DEVICES, 1, CAP, 2))(owner_keys, owner_turns).reshape((SLOTS, 1))
    block_pos = set_ends(jax.random.randint(splits[2], (SLOTS,), 0, TBLK), jax.random.fold_in(splits[2], 1), 0, TBLK - 1).astype(jnp.int32)
    omega = normal_values(splits[3], (N, RANK), N ** -0.5, 0.02734375, ((0, 4),))
    return {"blocks": blocks, "owner": owner, "block_pos": block_pos, "omega": omega}


def build_tile(sorted_blocks, sorted_pos, starts, counts, owner_index):
    window = DEVICES * CAP
    first_slot = starts[owner_index]
    chosen = lax.dynamic_slice_in_dim(sorted_blocks, first_slot, window, 0)
    placing = lax.dynamic_slice_in_dim(sorted_pos, first_slot, window, 0)
    active = jnp.arange(window, dtype=jnp.int32) < counts[owner_index]
    placing = jnp.where(active, placing, TBLK).astype(jnp.int32)
    summed = jnp.zeros((TBLK, BLK, BLK), jnp.float32).at[placing].add(chosen.astype(jnp.float32), mode='drop')
    rounded = lax.optimization_barrier(summed.astype(jnp.bfloat16))
    return rounded.astype(jnp.float32).reshape(PBR, TBC, BLK, BLK)

def reference(blocks, owner, block_pos, omega):
    target = owner[:, 0].astype(jnp.int32)
    ordering = jnp.argsort(target, stable=True)
    padding = DEVICES * CAP
    sorted_blocks = jnp.concatenate([blocks[ordering], jnp.zeros((padding, BLK, BLK), blocks.dtype)], 0)
    sorted_pos = jnp.concatenate([block_pos[ordering].astype(jnp.int32), jnp.zeros((padding,), jnp.int32)], 0)
    counts = jax.ops.segment_sum(jnp.ones_like(target), target, DEVICES).astype(jnp.int32)
    starts = (jnp.cumsum(counts) - counts).astype(jnp.int32)
    omega_blocks = omega.astype(jnp.float32).reshape(N_COLS, TBC, BLK, RANK)

    def panel_sketch(panel_index):
        running = jnp.zeros((PBR, BLK, RANK), jnp.float32)
        for column_index in range(N_COLS):
            dense_tile = build_tile(sorted_blocks, sorted_pos, starts, counts, panel_index * N_COLS + column_index)
            running = running + jnp.einsum('pcij,cjr->pir', dense_tile, omega_blocks[column_index])
        return running.reshape(PANEL, RANK)
    sketch = lax.map(panel_sketch, jnp.arange(N_ROWS, dtype=jnp.int32)).reshape(M, RANK)
    gram_sum = jnp.dot(sketch.T.astype(jnp.float32), sketch.astype(jnp.float32), precision=lax.Precision.HIGHEST, preferred_element_type=jnp.float32)
    factor = jnp.linalg.cholesky(gram_sum / M)
    basis_full = lax.linalg.triangular_solve(factor, sketch, left_side=False, lower=True, transpose_a=True)
    basis_half = basis_full.astype(jnp.bfloat16)
    basis_blocks = basis_half.astype(jnp.float32).reshape(N_ROWS, PBR, BLK, RANK)
    scaling = 1.0 / math.sqrt(M)

    def accumulate(running, panel_index):
        pieces = []
        for column_index in range(N_COLS):
            dense_tile = build_tile(sorted_blocks, sorted_pos, starts, counts, panel_index * N_COLS + column_index)
            product = jnp.einsum('pir,pcij->rcj', basis_blocks[panel_index], dense_tile).reshape(RANK, TCOL) * scaling
            pieces.append(product)
        return (running + jnp.concatenate(pieces, 1), None)
    coefficients, _ = lax.scan(accumulate, jnp.zeros((RANK, N), jnp.float32), jnp.arange(N_ROWS, dtype=jnp.int32))
    return (basis_half, coefficients)
```

```python
import functools
import math

import jax
import jax.numpy as jnp
from jax import lax
from jax.experimental import pallas as pl
from jax.experimental.pallas import tpu as pltpu
from jax.sharding import PartitionSpec as P

PBR = 4
TBC = 104
BLK = 128
HIGHEST = lax.Precision.HIGHEST
MIB = 1 << 20


def bucket_kernel(place_ref, blocks_ref, out_ref, sem):
    count = blocks_ref.shape[0]

    def issue(slot, carry):
        pltpu.make_async_copy(blocks_ref.at[slot], out_ref.at[place_ref[slot]], sem).start()
        return carry

    lax.fori_loop(0, count, issue, 0)
    pltpu.make_async_copy(blocks_ref, out_ref.at[pl.ds(0, count)], sem).wait()


def bucket(place, blocks, slots):
    return pl.pallas_call(
        bucket_kernel,
        grid_spec=pltpu.PrefetchScalarGridSpec(
            num_scalar_prefetch=1,
            grid=(),
            in_specs=[pl.BlockSpec(memory_space=pl.ANY)],
            out_specs=pl.BlockSpec(memory_space=pl.ANY),
            scratch_shapes=[pltpu.SemaphoreType.DMA],
        ),
        out_shape=jax.ShapeDtypeStruct((slots,) + blocks.shape[1:], blocks.dtype),
        cost_estimate=pl.CostEstimate(flops=0, bytes_accessed=2 * blocks.size * 2, transcendentals=0),
        name="bucket",
    )(place, blocks)


def tile_kernel(code_ref, got_hbm, omega_hbm, tile_hbm, sketch_ref, got, omega, tile, total, sems):
    slots = got.shape[0]
    rows, cols = tile.shape
    get_blocks = pltpu.make_async_copy(got_hbm, got, sems.at[0])
    get_omega = pltpu.make_async_copy(omega_hbm, omega, sems.at[1])
    get_blocks.start()
    get_omega.start()

    def clear(step, carry):
        tile[pl.ds(pl.multiple_of(step * 16, 16), 16), :] = jnp.zeros((16, cols), tile.dtype)
        return carry

    lax.fori_loop(0, rows // 16, clear, 0)
    get_blocks.wait()

    def insert(step, carry):
        code = code_ref[step]
        slot = code & 255
        row = pl.multiple_of(((code >> 8) & 3) * BLK, BLK)
        col = pl.multiple_of(((code >> 10) & 127) * BLK, BLK)
        again = (code >> 17) & 1
        later = (code >> 18) & 1

        @pl.when(again == 0)
        def _():
            tile[pl.ds(row, BLK), pl.ds(col, BLK)] = got[slot]

        @pl.when(again == 1)
        def _():
            @pl.when(later == 0)
            def _():
                total[...] = got[code_ref[step - 1] & 255].astype(jnp.float32)

            value = total[...] + got[slot].astype(jnp.float32)
            total[...] = value
            tile[pl.ds(row, BLK), pl.ds(col, BLK)] = value.astype(tile.dtype)

        return carry

    lax.fori_loop(0, code_ref[slots], insert, 0)
    put_tile = pltpu.make_async_copy(tile, tile_hbm, sems.at[2])
    put_tile.start()
    get_omega.wait()
    sketch_ref[...] = jnp.zeros_like(sketch_ref)
    depth = 1024

    def multiply(step, carry):
        at = pl.ds(pl.multiple_of(step * depth, depth), depth)
        sketch_ref[...] += jnp.dot(tile[:, at], omega[at, :], preferred_element_type=jnp.float32)
        return carry

    lax.fori_loop(0, cols // depth, multiply, 0)
    put_tile.wait()


def tile_and_sketch(code, got, omega, rows, cols):
    slots, rank = got.shape[0], omega.shape[1]
    return pl.pallas_call(
        tile_kernel,
        grid_spec=pltpu.PrefetchScalarGridSpec(
            num_scalar_prefetch=1,
            grid=(),
            in_specs=[pl.BlockSpec(memory_space=pl.ANY)] * 2,
            out_specs=[
                pl.BlockSpec(memory_space=pl.ANY),
                pl.BlockSpec(memory_space=pltpu.VMEM),
            ],
            scratch_shapes=[
                pltpu.VMEM((slots, BLK, BLK), jnp.bfloat16),
                pltpu.VMEM((cols, rank), jnp.bfloat16),
                pltpu.VMEM((rows, cols), jnp.bfloat16),
                pltpu.VMEM((BLK, BLK), jnp.float32),
                pltpu.SemaphoreType.DMA((3,)),
            ],
        ),
        out_shape=[
            jax.ShapeDtypeStruct((rows, cols), jnp.bfloat16),
            jax.ShapeDtypeStruct((rows, rank), jnp.float32),
        ],
        compiler_params=pltpu.CompilerParams(vmem_limit_bytes=52 * MIB),
        cost_estimate=pl.CostEstimate(
            flops=2 * rows * cols * rank,
            bytes_accessed=2 * (got.size + omega.size + rows * cols),
            transcendentals=0,
        ),
        name="tile_and_sketch",
    )(code, got, omega)


def factor_kernel(scale, gram_ref, out_ref, work):
    n = gram_ref.shape[0]
    work[...] = gram_ref[...] * scale
    row = lax.broadcasted_iota(jnp.int32, (n, n), 0)
    lane = lax.broadcasted_iota(jnp.int32, (n, n), 1)
    out_ref[...] = jnp.where(row == lane, 1.0, 0.0)
    sub = lax.broadcasted_iota(jnp.int32, (8, BLK), 0)
    lane8 = lax.broadcasted_iota(jnp.int32, (8, BLK), 1)
    groups = BLK // 8

    def block(k, carry):
        at = pl.ds(pl.multiple_of(k * BLK, BLK), BLK)
        left = [work[pl.ds(pl.multiple_of(k * BLK + 8 * g, 8), 8), at] for g in range(groups)]
        right = [jnp.where(lane8 == sub + 8 * g, 1.0, 0.0) for g in range(groups)]
        for j in range(BLK):
            g0, s0 = divmod(j, 8)
            columns = [
                jnp.broadcast_to(left[g][:, j : j + 1], (8, BLK)) for g in range(g0, groups)
            ]
            inverse = 1.0 / columns[0][s0 : s0 + 1, :]
            pivot_left = left[g0][s0 : s0 + 1, :] * inverse
            pivot_right = right[g0][s0 : s0 + 1, :] * inverse
            for g in range(g0, groups):
                column = columns[g - g0]
                if g == g0:
                    column = jnp.where(sub > s0, column, 0.0)
                left[g] = left[g] - column * pivot_left
                right[g] = right[g] - column * pivot_right
        halves = []
        for g in range(groups):
            pivot = jnp.sum(
                jnp.where(lane8 == sub + 8 * g, left[g], 0.0), axis=1, keepdims=True
            )
            halves.append(right[g] * (1.0 / jnp.sqrt(pivot)))
        inverse_block = jnp.concatenate(halves, axis=0)
        both = jnp.concatenate([work[at, :], out_ref[at, :]], axis=1)
        upper = jnp.dot(inverse_block, both, precision=HIGHEST, preferred_element_type=jnp.float32)
        lanes = lax.broadcasted_iota(jnp.int32, (BLK, n), 1)
        later = jnp.where(lanes >= (k + 1) * BLK, upper[:, :n], 0.0)
        change = lax.dot_general(
            later, upper, (((0,), (0,)), ((), ())), precision=HIGHEST, preferred_element_type=jnp.float32
        )
        work[...] -= change[:, :n]
        out_ref[...] -= change[:, n:]
        out_ref[at, :] = upper[:, n:]
        return carry

    lax.fori_loop(0, n // BLK, block, 0)


def inverse_factor(gram, scale):
    n = gram.shape[0]
    return pl.pallas_call(
        functools.partial(factor_kernel, scale),
        in_specs=[pl.BlockSpec(memory_space=pltpu.VMEM)],
        out_specs=pl.BlockSpec(memory_space=pltpu.VMEM),
        out_shape=jax.ShapeDtypeStruct((n, n), jnp.float32),
        scratch_shapes=[pltpu.VMEM((n, n), jnp.float32)],
        compiler_params=pltpu.CompilerParams(vmem_limit_bytes=24 * MIB),
        cost_estimate=pl.CostEstimate(
            flops=1 << 35, bytes_accessed=2 * n * n * 4, transcendentals=0
        ),
        name="inverse_factor",
    )(gram)


def product_kernel(left_ref, own_ref, other_ref, out_ref):
    rows = own_ref.shape[0]
    own, other = own_ref[...], other_ref[...]
    total = None
    for part in range(4):
        term = jnp.dot(
            left_ref[:, part * rows : (part + 1) * rows],
            own if part % 2 == 0 else other,
            preferred_element_type=jnp.float32,
        )
        total = term if total is None else total + term
    out_ref[0] = total


def product(left, own, other, chunks, width):
    rows, cols = own.shape
    half = left.shape[0]
    pair = 2 * cols // chunks
    step = pair // BLK // 2 * BLK

    def start(k):
        return pl.multiple_of((k // 2) * pair + (k % 2) * step, BLK)

    spec = pl.BlockSpec((pl.Element(rows), pl.Element(width)), lambda k: (0, start(k)))
    return pl.pallas_call(
        product_kernel,
        grid=(chunks,),
        in_specs=[pl.BlockSpec((half, 4 * rows), lambda k: (0, 0)), spec, spec],
        out_specs=pl.BlockSpec((1, half, width), lambda k: (k, 0, 0)),
        out_shape=jax.ShapeDtypeStruct((chunks, half, width), jnp.float32),
        compiler_params=pltpu.CompilerParams(vmem_limit_bytes=40 * MIB),
        cost_estimate=pl.CostEstimate(
            flops=2 * half * 4 * rows * chunks * width,
            bytes_accessed=4 * rows * cols + 4 * chunks * half * width,
            transcendentals=0,
        ),
        name="product",
    )(left, own, other)


def on_device(blocks, owner, block_pos, omega):
    slot_count = blocks.shape[0]
    rank = omega.shape[1]
    row_devices = lax.axis_size("rows")
    col_devices = lax.axis_size("cols")
    devices_all = row_devices * col_devices
    everywhere = ("rows", "cols")
    capacity = max(2, 2 * slot_count // devices_all)
    slots = devices_all * capacity
    panel, cols = PBR * BLK, TBC * BLK
    total_rows = panel * row_devices
    core = lax.axis_index("rows") % 2
    swap = [(i, i ^ 1) for i in range(row_devices)]

    target = owner[:, 0]
    numbers = jnp.arange(slot_count, dtype=jnp.int32)
    same = (target[:, None] == target[None, :]) & (numbers[None, :] < numbers[:, None])
    place = target * capacity + jnp.sum(same.astype(jnp.int32), axis=1)
    spots = jnp.arange(slots, dtype=jnp.int32)
    hit = place[None, :] == spots[:, None]
    send_where = jnp.sum(jnp.where(hit, block_pos[None, :] + 1, 0), axis=1)
    send_blocks = bucket(place, blocks, slots)
    got_blocks = lax.all_to_all(
        send_blocks.reshape(devices_all, capacity, BLK, BLK), everywhere, 0, 0, tiled=True
    ).reshape(slots, BLK, BLK)
    got_where = lax.all_to_all(
        send_where.reshape(devices_all, capacity), everywhere, 0, 0, tiled=True
    ).reshape(slots)

    key = jnp.where(got_where == 0, PBR * TBC, got_where - 1)
    before = (key[None, :] < key[:, None]) | (
        (key[None, :] == key[:, None]) & (spots[None, :] < spots[:, None])
    )
    order = jnp.sum(before.astype(jnp.int32), axis=1)
    packed = key * slots + spots
    ordered = jnp.sum(jnp.where(order[None, :] == spots[:, None], packed[None, :], 0), axis=1)
    slot, where = ordered % slots, ordered // slots
    again = jnp.concatenate([jnp.zeros((1,), jnp.int32), (where[1:] == where[:-1]).astype(jnp.int32)])
    later = jnp.concatenate([jnp.zeros((1,), jnp.int32), again[:-1]])
    code = slot + (where // TBC) * 256 + (where % TBC) * 1024 + (again << 17) + (later << 18)
    filled = jnp.sum((key < PBR * TBC).astype(jnp.int32))
    code = jnp.concatenate([code, filled[None]])

    tile, part = tile_and_sketch(code, got_blocks, omega, panel, cols)
    other_tile = lax.ppermute(tile, "rows", swap)

    share = panel // col_devices
    parts = lax.all_to_all(part.reshape(col_devices, share, rank), "cols", 0, 0, tiled=True)
    own_share = jnp.sum(parts, axis=0)
    local_gram = lax.dot_general(
        own_share, own_share, (((0,), (0,)), ((), ())), precision=HIGHEST, preferred_element_type=jnp.float32
    )
    grams = lax.all_to_all(
        local_gram.reshape(devices_all, rank // devices_all, rank), everywhere, 0, 0, tiled=True
    )
    gram_rows = jnp.sum(grams, axis=0)
    gram = lax.all_to_all(
        jnp.broadcast_to(gram_rows[None], (devices_all,) + gram_rows.shape), everywhere, 0, 0, tiled=True
    ).reshape(rank, rank)
    inverse = inverse_factor(gram, 1.0 / total_rows)

    sketch = lax.all_to_all(
        jnp.broadcast_to(own_share[None], (col_devices, share, rank)), "cols", 0, 0, tiled=True
    ).reshape(panel, rank)
    half = rank // 2
    mine = lax.dynamic_slice_in_dim(sketch, core * half, half, 1)
    theirs = lax.ppermute(lax.dynamic_slice_in_dim(sketch, (1 - core) * half, half, 1), "rows", swap)
    both = jnp.concatenate([mine, theirs], axis=0).T
    high = lax.reduce_precision(both, 8, 7)
    left = jnp.concatenate([high, both - high], axis=1).astype(jnp.bfloat16)

    chips = row_devices // 2
    width = -(-TBC // chips) * BLK
    terms = product(left, tile, other_tile, chips, width)
    groups = [[2 * i + c for i in range(chips)] for c in range(2)]
    summed = lax.psum_scatter(
        terms.reshape(chips * half, width), "rows", scatter_dimension=0, axis_index_groups=groups, tiled=True
    )
    quarter = width // BLK // 2 * BLK
    take = width - quarter
    kept = lax.dynamic_slice_in_dim(summed, core * quarter, take, 1)
    come = lax.ppermute(
        lax.dynamic_slice_in_dim(summed, (1 - core) * quarter, take, 1), "rows", swap
    )
    columns = jnp.where(
        core == 0, jnp.concatenate([kept, come], axis=0), jnp.concatenate([come, kept], axis=0)
    )
    solved = jnp.dot(
        inverse * (1.0 / math.sqrt(total_rows)), columns, precision=HIGHEST, preferred_element_type=jnp.float32
    )
    ranks = rank // row_devices
    pieces = lax.all_to_all(
        solved.reshape(row_devices, ranks, take), "rows", 0, 0, tiled=True
    ).reshape(row_devices // 4, 4, ranks, take)
    overlap = 4 * take - 4 * cols // row_devices
    skip = overlap // 3
    run = jnp.concatenate(
        [pieces[:, 0]] + [pieces[:, i, :, skip:] for i in range(1, 4)], axis=2
    )
    coefficients = run.transpose(1, 0, 2).reshape(ranks, cols)

    slice_width = rank // col_devices
    my_rows = lax.dynamic_slice_in_dim(inverse, lax.axis_index("cols") * slice_width, slice_width, 0)
    basis = lax.dot_general(
        sketch, my_rows, (((1,), (1,)), ((), ())), precision=HIGHEST, preferred_element_type=jnp.float32
    ).astype(jnp.bfloat16)
    return basis, coefficients


def solution(mesh):
    in_specs = (
        P(("rows", "cols"), None, None),
        P(("rows", "cols"), None),
        P(("rows", "cols")),
        P("cols", None),
    )
    out_specs = (P("rows", "cols"), P("rows", "cols"))
    return jax.shard_map(
        on_device, mesh=mesh, in_specs=in_specs, out_specs=out_specs, check_vma=False
    )
```

```python
import functools
import math

import jax
import jax.numpy as jnp
from jax import lax
from jax.experimental import pallas as pl
from jax.experimental.pallas import tpu as pltpu
from jax.sharding import PartitionSpec as P

PBR = 4
TBC = 104
BLK = 128
HIGHEST = lax.Precision.HIGHEST
MIB = 1 << 20


def bucket_kernel(place_ref, blocks_ref, out_ref, sem):
    count = blocks_ref.shape[0]

    def issue(slot, carry):
        pltpu.make_async_copy(blocks_ref.at[slot], out_ref.at[place_ref[slot]], sem).start()
        return carry

    lax.fori_loop(0, count, issue, 0)
    pltpu.make_async_copy(blocks_ref, out_ref.at[pl.ds(0, count)], sem).wait()


def bucket(place, blocks, slots):
    return pl.pallas_call(
        bucket_kernel,
        grid_spec=pltpu.PrefetchScalarGridSpec(
            num_scalar_prefetch=1,
            grid=(),
            in_specs=[pl.BlockSpec(memory_space=pltpu.VMEM)],
            out_specs=pl.BlockSpec(memory_space=pl.ANY),
            scratch_shapes=[pltpu.SemaphoreType.DMA],
        ),
        out_shape=jax.ShapeDtypeStruct((slots,) + blocks.shape[1:], blocks.dtype),
        compiler_params=pltpu.CompilerParams(vmem_limit_bytes=56 * MIB),
        cost_estimate=pl.CostEstimate(flops=0, bytes_accessed=2 * blocks.size * 2, transcendentals=0),
        name="bucket",
    )(place, blocks)


def tile_kernel(code_ref, got_hbm, omega_hbm, tile_hbm, sketch_ref, got, omega, tile, total, sems):
    slots = got.shape[0]
    rows, cols = tile.shape
    get_blocks = pltpu.make_async_copy(got_hbm, got, sems.at[0])
    get_omega = pltpu.make_async_copy(omega_hbm, omega, sems.at[1])
    get_blocks.start()
    get_omega.start()

    def clear(step, carry):
        tile[pl.ds(pl.multiple_of(step * 16, 16), 16), :] = jnp.zeros((16, cols), tile.dtype)
        return carry

    lax.fori_loop(0, rows // 16, clear, 0)
    get_blocks.wait()

    def insert(step, carry):
        code = code_ref[step]
        slot = code & 255
        row = pl.multiple_of(((code >> 8) & 3) * BLK, BLK)
        col = pl.multiple_of(((code >> 10) & 127) * BLK, BLK)
        again = (code >> 17) & 1
        later = (code >> 18) & 1

        @pl.when(again == 0)
        def _():
            tile[pl.ds(row, BLK), pl.ds(col, BLK)] = got[slot]

        @pl.when(again == 1)
        def _():
            @pl.when(later == 0)
            def _():
                total[...] = got[code_ref[step - 1] & 255].astype(jnp.float32)

            value = total[...] + got[slot].astype(jnp.float32)
            total[...] = value
            tile[pl.ds(row, BLK), pl.ds(col, BLK)] = value.astype(tile.dtype)

        return carry

    lax.fori_loop(0, code_ref[slots], insert, 0)
    put_tile = pltpu.make_async_copy(tile, tile_hbm, sems.at[2])
    put_tile.start()
    get_omega.wait()
    sketch_ref[...] = jnp.zeros_like(sketch_ref)
    depth = 1024

    def multiply(step, carry):
        at = pl.ds(pl.multiple_of(step * depth, depth), depth)
        sketch_ref[...] += jnp.dot(tile[:, at], omega[at, :], preferred_element_type=jnp.float32)
        return carry

    lax.fori_loop(0, cols // depth, multiply, 0)
    put_tile.wait()


def tile_and_sketch(code, got, omega, rows, cols):
    slots, rank = got.shape[0], omega.shape[1]
    return pl.pallas_call(
        tile_kernel,
        grid_spec=pltpu.PrefetchScalarGridSpec(
            num_scalar_prefetch=1,
            grid=(),
            in_specs=[pl.BlockSpec(memory_space=pl.ANY)] * 2,
            out_specs=[
                pl.BlockSpec(memory_space=pl.ANY),
                pl.BlockSpec(memory_space=pltpu.VMEM),
            ],
            scratch_shapes=[
                pltpu.VMEM((slots, BLK, BLK), jnp.bfloat16),
                pltpu.VMEM((cols, rank), jnp.bfloat16),
                pltpu.VMEM((rows, cols), jnp.bfloat16),
                pltpu.VMEM((BLK, BLK), jnp.float32),
                pltpu.SemaphoreType.DMA((3,)),
            ],
        ),
        out_shape=[
            jax.ShapeDtypeStruct((rows, cols), jnp.bfloat16),
            jax.ShapeDtypeStruct((rows, rank), jnp.float32),
        ],
        compiler_params=pltpu.CompilerParams(vmem_limit_bytes=52 * MIB),
        cost_estimate=pl.CostEstimate(
            flops=2 * rows * cols * rank,
            bytes_accessed=2 * (got.size + omega.size + rows * cols),
            transcendentals=0,
        ),
        name="tile_and_sketch",
    )(code, got, omega)


def factor_kernel(scale, gram_ref, out_ref, work):
    n = gram_ref.shape[0]
    work[...] = gram_ref[...] * scale
    row = lax.broadcasted_iota(jnp.int32, (n, n), 0)
    lane = lax.broadcasted_iota(jnp.int32, (n, n), 1)
    out_ref[...] = jnp.where(row == lane, 1.0, 0.0)
    sub = lax.broadcasted_iota(jnp.int32, (8, BLK), 0)
    lane8 = lax.broadcasted_iota(jnp.int32, (8, BLK), 1)
    groups = BLK // 8

    def spread(value, j):
        return jnp.broadcast_to(value[:, j : j + 1], (8, BLK))

    def block(panel, carry):
        at = pl.ds(pl.multiple_of(panel * BLK, BLK), BLK)
        left = [work[pl.ds(pl.multiple_of(panel * BLK + 8 * g, 8), 8), at] for g in range(groups)]
        right = [jnp.where(lane8 == sub + 8 * g, 1.0, 0.0) for g in range(groups)]
        for g0 in range(groups):
            own = [spread(left[g0], 8 * g0 + k) for k in range(8)]
            factors, pivots_left, pivots_right = {}, [], []
            for k in range(8):
                inverse = 1.0 / own[k][k : k + 1, :]
                for later in range(k + 1, 8):
                    factors[k, later] = own[later][k : k + 1, :] * inverse
                    own[later] = own[later] - own[k] * factors[k, later]
                pivots_left.append(left[g0][k : k + 1, :] * inverse)
                pivots_right.append(right[g0][k : k + 1, :] * inverse)
                column = jnp.where(sub > k, own[k], 0.0)
                left[g0] = left[g0] - column * pivots_left[k]
                right[g0] = right[g0] - column * pivots_right[k]
            for g in range(g0 + 1, groups):
                below = [spread(left[g], 8 * g0 + k) for k in range(8)]
                for k in range(8):
                    for later in range(k + 1, 8):
                        below[later] = below[later] - below[k] * factors[k, later]
                    left[g] = left[g] - below[k] * pivots_left[k]
                    right[g] = right[g] - below[k] * pivots_right[k]
        halves = []
        for g in range(groups):
            pivot = jnp.sum(
                jnp.where(lane8 == sub + 8 * g, left[g], 0.0), axis=1, keepdims=True
            )
            halves.append(right[g] * (1.0 / jnp.sqrt(pivot)))
        inverse_block = jnp.concatenate(halves, axis=0)
        both = jnp.concatenate([work[at, :], out_ref[at, :]], axis=1)
        upper = jnp.dot(inverse_block, both, precision=HIGHEST, preferred_element_type=jnp.float32)

        @pl.when(panel < n // BLK - 1)
        def _():
            lanes = lax.broadcasted_iota(jnp.int32, (BLK, n), 1)
            later = jnp.where(lanes >= (panel + 1) * BLK, upper[:, :n], 0.0)
            change = lax.dot_general(
                later, upper, (((0,), (0,)), ((), ())), precision=HIGHEST, preferred_element_type=jnp.float32
            )
            work[...] -= change[:, :n]
            out_ref[...] -= change[:, n:]

        out_ref[at, :] = upper[:, n:]
        return carry

    lax.fori_loop(0, n // BLK, block, 0)


def inverse_factor(gram, scale):
    n = gram.shape[0]
    return pl.pallas_call(
        functools.partial(factor_kernel, scale),
        in_specs=[pl.BlockSpec(memory_space=pltpu.VMEM)],
        out_specs=pl.BlockSpec(memory_space=pltpu.VMEM),
        out_shape=jax.ShapeDtypeStruct((n, n), jnp.float32),
        scratch_shapes=[pltpu.VMEM((n, n), jnp.float32)],
        compiler_params=pltpu.CompilerParams(vmem_limit_bytes=24 * MIB),
        cost_estimate=pl.CostEstimate(
            flops=1 << 35, bytes_accessed=2 * n * n * 4, transcendentals=0
        ),
        name="inverse_factor",
    )(gram)


def product_kernel(left_ref, own_ref, other_ref, out_ref):
    rows = own_ref.shape[0]
    total = jnp.dot(left_ref[:, :rows], own_ref[...], preferred_element_type=jnp.float32)
    total += jnp.dot(left_ref[:, rows:], other_ref[...], preferred_element_type=jnp.float32)
    out_ref[...] = total.astype(out_ref.dtype)


def product(left, own, other, part, parts, width):
    rows, cols = own.shape
    half = left.shape[0]
    steps = cols // parts // width
    spec = pl.BlockSpec((rows, width), lambda k: (0, part * steps + k))
    return pl.pallas_call(
        product_kernel,
        grid=(steps,),
        in_specs=[pl.BlockSpec((half, 2 * rows), lambda k: (0, 0)), spec, spec],
        out_specs=pl.BlockSpec((half, width), lambda k: (0, k)),
        out_shape=jax.ShapeDtypeStruct((half, cols // parts), jnp.bfloat16),
        compiler_params=pltpu.CompilerParams(vmem_limit_bytes=56 * MIB),
        cost_estimate=pl.CostEstimate(
            flops=2 * half * 2 * rows * cols // parts,
            bytes_accessed=(4 * rows * cols + 2 * half * cols) // parts,
            transcendentals=0,
        ),
        name="product",
    )(left, own, other)


def on_device(blocks, owner, block_pos, omega):
    slot_count = blocks.shape[0]
    rank = omega.shape[1]
    row_devices = lax.axis_size("rows")
    col_devices = lax.axis_size("cols")
    devices_all = row_devices * col_devices
    everywhere = ("rows", "cols")
    capacity = max(2, 2 * slot_count // devices_all)
    slots = devices_all * capacity
    panel, cols = PBR * BLK, TBC * BLK
    total_rows = panel * row_devices
    core = lax.axis_index("rows") % 2
    swap = [(i, i ^ 1) for i in range(row_devices)]

    target = owner[:, 0]
    numbers = jnp.arange(slot_count, dtype=jnp.int32)
    same = (target[:, None] == target[None, :]) & (numbers[None, :] < numbers[:, None])
    place = target * capacity + jnp.sum(same.astype(jnp.int32), axis=1)
    spots = jnp.arange(slots, dtype=jnp.int32)
    hit = place[None, :] == spots[:, None]
    send_where = jnp.sum(jnp.where(hit, block_pos[None, :] + 1, 0), axis=1)
    send_blocks, send_where = lax.optimization_barrier((bucket(place, blocks, slots), send_where))
    got_blocks = lax.all_to_all(
        send_blocks.reshape(devices_all, capacity, BLK, BLK), everywhere, 0, 0, tiled=True
    ).reshape(slots, BLK, BLK)
    got_where = lax.all_to_all(
        send_where.reshape(devices_all, capacity), everywhere, 0, 0, tiled=True
    ).reshape(slots)

    key = jnp.where(got_where == 0, PBR * TBC, got_where - 1)
    before = (key[None, :] < key[:, None]) | (
        (key[None, :] == key[:, None]) & (spots[None, :] < spots[:, None])
    )
    order = jnp.sum(before.astype(jnp.int32), axis=1)
    packed = key * slots + spots
    ordered = jnp.sum(jnp.where(order[None, :] == spots[:, None], packed[None, :], 0), axis=1)
    slot, where = ordered % slots, ordered // slots
    again = jnp.concatenate([jnp.zeros((1,), jnp.int32), (where[1:] == where[:-1]).astype(jnp.int32)])
    later = jnp.concatenate([jnp.zeros((1,), jnp.int32), again[:-1]])
    code = slot + (where // TBC) * 256 + (where % TBC) * 1024 + (again << 17) + (later << 18)
    filled = jnp.sum((key < PBR * TBC).astype(jnp.int32))
    code = jnp.concatenate([code, filled[None]])

    tile, part = tile_and_sketch(code, got_blocks, omega, panel, cols)
    other_tile = lax.ppermute(tile, "rows", swap)

    share = panel // col_devices
    parts = lax.all_to_all(part.reshape(col_devices, share, rank), "cols", 0, 0, tiled=True)
    own_share = jnp.sum(parts, axis=0)
    local_gram = lax.dot_general(
        own_share, own_share, (((0,), (0,)), ((), ())), precision=HIGHEST, preferred_element_type=jnp.float32
    )
    grams = lax.all_to_all(
        local_gram.reshape(devices_all, rank // devices_all, rank), everywhere, 0, 0, tiled=True
    )
    gram_rows = jnp.sum(grams, axis=0)
    gram = lax.all_to_all(
        jnp.broadcast_to(gram_rows[None], (devices_all,) + gram_rows.shape), everywhere, 0, 0, tiled=True
    ).reshape(rank, rank)
    shares = [own_share] + [
        lax.ppermute(own_share, "cols", [(i, (i + d) % col_devices) for i in range(col_devices)])
        for d in range(1, col_devices)
    ]
    back = jnp.stack(shares[::-1] * 2)
    start = col_devices - 1 - lax.axis_index("cols")
    sketch = lax.dynamic_slice_in_dim(back, start, col_devices, 0).reshape(panel, rank)
    other_sketch = lax.ppermute(sketch, "rows", swap)
    inverse = inverse_factor(gram, 1.0 / total_rows)

    ranks = rank // row_devices
    half = rank // 2
    chips = row_devices // 2
    both = jnp.concatenate([sketch, other_sketch], axis=0)
    my_ranks = lax.dynamic_index_in_dim(
        inverse.reshape(chips, 2, ranks, rank), core, 1, keepdims=False
    ).reshape(half, rank)
    left = lax.dot_general(
        my_ranks, both, (((1,), (1,)), ((), ())), precision=HIGHEST, preferred_element_type=jnp.float32
    ).astype(jnp.bfloat16)

    groups = [[2 * i + c for i in range(chips)] for c in range(2)]
    scaling = 1.0 / math.sqrt(total_rows)
    halves = []
    for part in range(2):
        terms = product(left, tile, other_tile, part, 2, 512).reshape(chips, ranks, cols // 2)
        terms = lax.all_to_all(terms, "rows", 0, 0, axis_index_groups=groups, tiled=True)
        halves.append(jnp.sum(terms.astype(jnp.float32), axis=0) * scaling)
    coefficients = jnp.concatenate(halves, axis=1)

    slice_width = rank // col_devices
    my_rows = lax.dynamic_slice_in_dim(inverse, lax.axis_index("cols") * slice_width, slice_width, 0)
    basis = lax.dot_general(
        sketch, my_rows, (((1,), (1,)), ((), ())), precision=HIGHEST, preferred_element_type=jnp.float32
    ).astype(jnp.bfloat16)
    return basis, coefficients


def solution(mesh):
    in_specs = (
        P(("rows", "cols"), None, None),
        P(("rows", "cols"), None),
        P(("rows", "cols")),
        P("cols", None),
    )
    out_specs = (P("rows", "cols"), P("rows", "cols"))
    return jax.shard_map(
        on_device, mesh=mesh, in_specs=in_specs, out_specs=out_specs, check_vma=False
    )
```

```python
import functools
import math

import jax
import jax.numpy as jnp
from jax import lax
from jax.experimental import pallas as pl
from jax.experimental.pallas import tpu as pltpu
from jax.sharding import PartitionSpec as P

PBR = 4
TBC = 104
BLK = 128
HIGHEST = lax.Precision.HIGHEST
MIB = 1 << 20


def bucket_kernel(place_ref, blocks_ref, out_ref, sem):
    count = blocks_ref.shape[0]

    def issue(slot, carry):
        pltpu.make_async_copy(blocks_ref.at[slot], out_ref.at[place_ref[slot]], sem).start()
        return carry

    lax.fori_loop(0, count, issue, 0)
    pltpu.make_async_copy(blocks_ref, out_ref.at[pl.ds(0, count)], sem).wait()


def bucket(place, blocks, slots):
    return pl.pallas_call(
        bucket_kernel,
        grid_spec=pltpu.PrefetchScalarGridSpec(
            num_scalar_prefetch=1,
            grid=(),
            in_specs=[pl.BlockSpec(memory_space=pltpu.VMEM)],
            out_specs=pl.BlockSpec(memory_space=pl.ANY),
            scratch_shapes=[pltpu.SemaphoreType.DMA],
        ),
        out_shape=jax.ShapeDtypeStruct((slots,) + blocks.shape[1:], blocks.dtype),
        compiler_params=pltpu.CompilerParams(vmem_limit_bytes=56 * MIB),
        cost_estimate=pl.CostEstimate(flops=0, bytes_accessed=2 * blocks.size * 2, transcendentals=0),
        name="bucket",
    )(place, blocks)


def tile_kernel(code_ref, got_hbm, omega_hbm, tile_hbm, sketch_ref, got, omega, tile, total, sems):
    slots = got.shape[0]
    rows, cols = tile.shape
    get_blocks = pltpu.make_async_copy(got_hbm, got, sems.at[0])
    get_omega = pltpu.make_async_copy(omega_hbm, omega, sems.at[1])
    get_blocks.start()
    get_omega.start()

    def clear(step, carry):
        tile[pl.ds(pl.multiple_of(step * 16, 16), 16), :] = jnp.zeros((16, cols), tile.dtype)
        return carry

    lax.fori_loop(0, rows // 16, clear, 0)
    get_blocks.wait()

    def insert(step, carry):
        code = code_ref[step]
        slot = code & 255
        row = pl.multiple_of(((code >> 8) & 3) * BLK, BLK)
        col = pl.multiple_of(((code >> 10) & 127) * BLK, BLK)
        again = (code >> 17) & 1
        later = (code >> 18) & 1

        @pl.when(again == 0)
        def _():
            tile[pl.ds(row, BLK), pl.ds(col, BLK)] = got[slot]

        @pl.when(again == 1)
        def _():
            @pl.when(later == 0)
            def _():
                total[...] = got[code_ref[step - 1] & 255].astype(jnp.float32)

            value = total[...] + got[slot].astype(jnp.float32)
            total[...] = value
            tile[pl.ds(row, BLK), pl.ds(col, BLK)] = value.astype(tile.dtype)

        return carry

    lax.fori_loop(0, code_ref[slots], insert, 0)
    put_tile = pltpu.make_async_copy(tile, tile_hbm, sems.at[2])
    put_tile.start()
    get_omega.wait()
    sketch_ref[...] = jnp.zeros_like(sketch_ref)
    depth = 1024

    def multiply(step, carry):
        at = pl.ds(pl.multiple_of(step * depth, depth), depth)
        sketch_ref[...] += jnp.dot(tile[:, at], omega[at, :], preferred_element_type=jnp.float32)
        return carry

    lax.fori_loop(0, cols // depth, multiply, 0)
    put_tile.wait()


def tile_and_sketch(code, got, omega, rows, cols):
    slots, rank = got.shape[0], omega.shape[1]
    return pl.pallas_call(
        tile_kernel,
        grid_spec=pltpu.PrefetchScalarGridSpec(
            num_scalar_prefetch=1,
            grid=(),
            in_specs=[pl.BlockSpec(memory_space=pl.ANY)] * 2,
            out_specs=[
                pl.BlockSpec(memory_space=pl.ANY),
                pl.BlockSpec(memory_space=pltpu.VMEM),
            ],
            scratch_shapes=[
                pltpu.VMEM((slots, BLK, BLK), jnp.bfloat16),
                pltpu.VMEM((cols, rank), jnp.bfloat16),
                pltpu.VMEM((rows, cols), jnp.bfloat16),
                pltpu.VMEM((BLK, BLK), jnp.float32),
                pltpu.SemaphoreType.DMA((3,)),
            ],
        ),
        out_shape=[
            jax.ShapeDtypeStruct((rows, cols), jnp.bfloat16),
            jax.ShapeDtypeStruct((rows, rank), jnp.float32),
        ],
        compiler_params=pltpu.CompilerParams(vmem_limit_bytes=52 * MIB),
        cost_estimate=pl.CostEstimate(
            flops=2 * rows * cols * rank,
            bytes_accessed=2 * (got.size + omega.size + rows * cols),
            transcendentals=0,
        ),
        name="tile_and_sketch",
    )(code, got, omega)


def factor_kernel(scale, gram_ref, out_ref, work):
    n = gram_ref.shape[0]
    work[...] = gram_ref[...] * scale
    row = lax.broadcasted_iota(jnp.int32, (n, n), 0)
    lane = lax.broadcasted_iota(jnp.int32, (n, n), 1)
    out_ref[...] = jnp.where(row == lane, 1.0, 0.0)
    sub = lax.broadcasted_iota(jnp.int32, (8, BLK), 0)
    lane8 = lax.broadcasted_iota(jnp.int32, (8, BLK), 1)
    groups = BLK // 8

    def spread(value, j):
        return jnp.broadcast_to(value[:, j : j + 1], (8, BLK))

    def block(panel, carry):
        at = pl.ds(pl.multiple_of(panel * BLK, BLK), BLK)
        left = [work[pl.ds(pl.multiple_of(panel * BLK + 8 * g, 8), 8), at] for g in range(groups)]
        right = [jnp.where(lane8 == sub + 8 * g, 1.0, 0.0) for g in range(groups)]
        for g0 in range(groups):
            own = [spread(left[g0], 8 * g0 + k) for k in range(8)]
            factors, pivots_left, pivots_right = {}, [], []
            for k in range(8):
                inverse = 1.0 / own[k][k : k + 1, :]
                for later in range(k + 1, 8):
                    factors[k, later] = own[later][k : k + 1, :] * inverse
                    own[later] = own[later] - own[k] * factors[k, later]
                pivots_left.append(left[g0][k : k + 1, :] * inverse)
                pivots_right.append(right[g0][k : k + 1, :] * inverse)
                column = jnp.where(sub > k, own[k], 0.0)
                left[g0] = left[g0] - column * pivots_left[k]
                right[g0] = right[g0] - column * pivots_right[k]
            for g in range(g0 + 1, groups):
                below = [spread(left[g], 8 * g0 + k) for k in range(8)]
                for k in range(8):
                    for later in range(k + 1, 8):
                        below[later] = below[later] - below[k] * factors[k, later]
                    left[g] = left[g] - below[k] * pivots_left[k]
                    right[g] = right[g] - below[k] * pivots_right[k]
        halves = []
        for g in range(groups):
            pivot = jnp.sum(
                jnp.where(lane8 == sub + 8 * g, left[g], 0.0), axis=1, keepdims=True
            )
            halves.append(right[g] * (1.0 / jnp.sqrt(pivot)))
        inverse_block = jnp.concatenate(halves, axis=0)
        both = jnp.concatenate([work[at, :], out_ref[at, :]], axis=1)
        upper = jnp.dot(inverse_block, both, precision=HIGHEST, preferred_element_type=jnp.float32)

        @pl.when(panel < n // BLK - 1)
        def _():
            lanes = lax.broadcasted_iota(jnp.int32, (BLK, n), 1)
            later = jnp.where(lanes >= (panel + 1) * BLK, upper[:, :n], 0.0)
            change = lax.dot_general(
                later, upper, (((0,), (0,)), ((), ())), precision=HIGHEST, preferred_element_type=jnp.float32
            )
            work[...] -= change[:, :n]
            out_ref[...] -= change[:, n:]

        out_ref[at, :] = upper[:, n:]
        return carry

    lax.fori_loop(0, n // BLK, block, 0)


def inverse_factor(gram, scale):
    n = gram.shape[0]
    return pl.pallas_call(
        functools.partial(factor_kernel, scale),
        in_specs=[pl.BlockSpec(memory_space=pltpu.VMEM)],
        out_specs=pl.BlockSpec(memory_space=pltpu.VMEM),
        out_shape=jax.ShapeDtypeStruct((n, n), jnp.float32),
        scratch_shapes=[pltpu.VMEM((n, n), jnp.float32)],
        compiler_params=pltpu.CompilerParams(vmem_limit_bytes=24 * MIB),
        cost_estimate=pl.CostEstimate(
            flops=1 << 35, bytes_accessed=2 * n * n * 4, transcendentals=0
        ),
        name="inverse_factor",
    )(gram)


def product_kernel(left_ref, own_ref, other_ref, out_ref):
    rows = own_ref.shape[0]
    total = jnp.dot(left_ref[:, :rows], own_ref[...], preferred_element_type=jnp.float32)
    total += jnp.dot(left_ref[:, rows:], other_ref[...], preferred_element_type=jnp.float32)
    out_ref[...] = total.astype(out_ref.dtype)


def product(left, own, other, width):
    rows, cols = own.shape
    half = left.shape[0]
    spec = pl.BlockSpec((rows, width), lambda k: (0, k))
    return pl.pallas_call(
        product_kernel,
        grid=(cols // width,),
        in_specs=[pl.BlockSpec((half, 2 * rows), lambda k: (0, 0)), spec, spec],
        out_specs=pl.BlockSpec((half, width), lambda k: (0, k)),
        out_shape=jax.ShapeDtypeStruct((half, cols), jnp.bfloat16),
        compiler_params=pltpu.CompilerParams(vmem_limit_bytes=56 * MIB),
        cost_estimate=pl.CostEstimate(
            flops=2 * half * 2 * rows * cols,
            bytes_accessed=4 * rows * cols + 2 * half * cols,
            transcendentals=0,
        ),
        name="product",
    )(left, own, other)


def on_device(blocks, owner, block_pos, omega):
    slot_count = blocks.shape[0]
    rank = omega.shape[1]
    row_devices = lax.axis_size("rows")
    col_devices = lax.axis_size("cols")
    devices_all = row_devices * col_devices
    everywhere = ("rows", "cols")
    capacity = max(2, 2 * slot_count // devices_all)
    slots = devices_all * capacity
    panel, cols = PBR * BLK, TBC * BLK
    total_rows = panel * row_devices
    core = lax.axis_index("rows") % 2
    swap = [(i, i ^ 1) for i in range(row_devices)]

    target = owner[:, 0]
    numbers = jnp.arange(slot_count, dtype=jnp.int32)
    same = (target[:, None] == target[None, :]) & (numbers[None, :] < numbers[:, None])
    place = target * capacity + jnp.sum(same.astype(jnp.int32), axis=1)
    send_blocks, listed = lax.optimization_barrier(
        (bucket(place, blocks, slots), target * PBR * TBC + block_pos)
    )
    got_blocks = lax.all_to_all(
        send_blocks.reshape(devices_all, capacity, BLK, BLK), everywhere, 0, 0, tiled=True
    ).reshape(slots, BLK, BLK)

    listed = lax.all_gather(listed, everywhere, axis=0)
    me = lax.axis_index("rows") * col_devices + lax.axis_index("cols")
    place_here = listed - me * PBR * TBC
    here = (place_here >= 0) & (place_here < PBR * TBC)
    first = jnp.min(jnp.where(here, numbers[None, :], slot_count), axis=1)
    last = jnp.max(jnp.where(here, numbers[None, :], -1), axis=1)
    taken = jnp.where(here, place_here + 1, 0)
    first_where = jnp.sum(jnp.where(numbers[None, :] == first[:, None], taken, 0), axis=1)
    last_where = jnp.sum(jnp.where(numbers[None, :] == last[:, None], taken, 0), axis=1)
    got_where = jnp.stack([first_where, jnp.where(last > first, last_where, 0)], axis=1).reshape(slots)

    spots = jnp.arange(slots, dtype=jnp.int32)
    key = jnp.where(got_where == 0, PBR * TBC, got_where - 1)
    before = (key[None, :] < key[:, None]) | (
        (key[None, :] == key[:, None]) & (spots[None, :] < spots[:, None])
    )
    order = jnp.sum(before.astype(jnp.int32), axis=1)
    packed = key * slots + spots
    ordered = jnp.sum(jnp.where(order[None, :] == spots[:, None], packed[None, :], 0), axis=1)
    slot, where = ordered % slots, ordered // slots
    again = jnp.concatenate([jnp.zeros((1,), jnp.int32), (where[1:] == where[:-1]).astype(jnp.int32)])
    later = jnp.concatenate([jnp.zeros((1,), jnp.int32), again[:-1]])
    code = slot + (where // TBC) * 256 + (where % TBC) * 1024 + (again << 17) + (later << 18)
    filled = jnp.sum((key < PBR * TBC).astype(jnp.int32))
    code = jnp.concatenate([code, filled[None]])

    tile, part = tile_and_sketch(code, got_blocks, omega, panel, cols)
    other_tile = lax.ppermute(tile, "rows", swap)

    share = panel // col_devices
    parts = lax.all_to_all(part.reshape(col_devices, share, rank), "cols", 0, 0, tiled=True)
    own_share = jnp.sum(parts, axis=0)
    local_gram = lax.dot_general(
        own_share, own_share, (((0,), (0,)), ((), ())), precision=HIGHEST, preferred_element_type=jnp.float32
    )
    grams = lax.all_to_all(
        local_gram.reshape(devices_all, rank // devices_all, rank), everywhere, 0, 0, tiled=True
    )
    gram_rows, late_share = lax.optimization_barrier((jnp.sum(grams, axis=0), own_share))
    gram = lax.all_to_all(
        jnp.broadcast_to(gram_rows[None], (devices_all,) + gram_rows.shape), everywhere, 0, 0, tiled=True
    ).reshape(rank, rank)
    shares = [late_share] + [
        lax.ppermute(late_share, "cols", [(i, (i + d) % col_devices) for i in range(col_devices)])
        for d in range(1, col_devices)
    ]
    back = jnp.stack(shares[::-1] * 2)
    start = col_devices - 1 - lax.axis_index("cols")
    sketch = lax.dynamic_slice_in_dim(back, start, col_devices, 0).reshape(panel, rank)
    other_sketch = lax.ppermute(sketch, "rows", swap)
    inverse = inverse_factor(gram, 1.0 / total_rows)

    ranks = rank // row_devices
    half = rank // 2
    chips = row_devices // 2
    both = jnp.concatenate([sketch, other_sketch], axis=0)
    my_ranks = lax.dynamic_index_in_dim(
        inverse.reshape(chips, 2, ranks, rank), core, 1, keepdims=False
    ).reshape(half, rank)
    left = lax.dot_general(
        my_ranks, both, (((1,), (1,)), ((), ())), precision=HIGHEST, preferred_element_type=jnp.float32
    ).astype(jnp.bfloat16)

    groups = [[2 * i + c for i in range(chips)] for c in range(2)]
    scaling = 1.0 / math.sqrt(total_rows)
    terms = product(left, tile, other_tile, cols // 4).reshape(chips, ranks, cols)
    terms = lax.all_to_all(terms, "rows", 0, 0, axis_index_groups=groups, tiled=True)
    coefficients = jnp.sum(terms.astype(jnp.float32), axis=0) * scaling

    slice_width = rank // col_devices
    my_rows = lax.dynamic_slice_in_dim(inverse, lax.axis_index("cols") * slice_width, slice_width, 0)
    basis = lax.dot_general(
        sketch, my_rows, (((1,), (1,)), ((), ())), precision=HIGHEST, preferred_element_type=jnp.float32
    ).astype(jnp.bfloat16)
    return basis, coefficients


def solution(mesh):
    in_specs = (
        P(("rows", "cols"), None, None),
        P(("rows", "cols"), None),
        P(("rows", "cols")),
        P("cols", None),
    )
    out_specs = (P("rows", "cols"), P("rows", "cols"))
    return jax.shard_map(
        on_device, mesh=mesh, in_specs=in_specs, out_specs=out_specs, check_vma=False
    )
```

```python
import functools
import math

import jax
import jax.numpy as jnp
from jax import lax
from jax.experimental import pallas as pl
from jax.experimental.pallas import tpu as pltpu
from jax.sharding import PartitionSpec as P

PBR = 4
TBC = 104
BLK = 128
HIGHEST = lax.Precision.HIGHEST
MIB = 1 << 20


def bucket_kernel(place_ref, blocks_ref, out_ref, sem):
    count = blocks_ref.shape[0]

    def issue(slot, carry):
        pltpu.make_async_copy(blocks_ref.at[slot], out_ref.at[place_ref[slot]], sem).start()
        return carry

    lax.fori_loop(0, count, issue, 0)
    pltpu.make_async_copy(blocks_ref, out_ref.at[pl.ds(0, count)], sem).wait()


def bucket(place, blocks, slots):
    return pl.pallas_call(
        bucket_kernel,
        grid_spec=pltpu.PrefetchScalarGridSpec(
            num_scalar_prefetch=1,
            grid=(),
            in_specs=[pl.BlockSpec(memory_space=pltpu.VMEM)],
            out_specs=pl.BlockSpec(memory_space=pl.ANY),
            scratch_shapes=[pltpu.SemaphoreType.DMA],
        ),
        out_shape=jax.ShapeDtypeStruct((slots,) + blocks.shape[1:], blocks.dtype),
        compiler_params=pltpu.CompilerParams(vmem_limit_bytes=56 * MIB),
        cost_estimate=pl.CostEstimate(flops=0, bytes_accessed=2 * blocks.size * 2, transcendentals=0),
        name="bucket",
    )(place, blocks)


def tile_kernel(code_ref, got_hbm, omega_hbm, tile_hbm, sketch_ref, got, omega, tile, total, sems):
    slots = got.shape[0]
    rows, cols = tile.shape
    get_blocks = pltpu.make_async_copy(got_hbm, got, sems.at[0])
    get_omega = pltpu.make_async_copy(omega_hbm, omega, sems.at[1])
    get_blocks.start()
    get_omega.start()

    def clear(step, carry):
        tile[pl.ds(pl.multiple_of(step * 16, 16), 16), :] = jnp.zeros((16, cols), tile.dtype)
        return carry

    lax.fori_loop(0, rows // 16, clear, 0)
    get_blocks.wait()

    def insert(step, carry):
        code = code_ref[step]
        slot = code & 255
        row = pl.multiple_of(((code >> 8) & 3) * BLK, BLK)
        col = pl.multiple_of(((code >> 10) & 127) * BLK, BLK)
        again = (code >> 17) & 1
        later = (code >> 18) & 1

        @pl.when(again == 0)
        def _():
            tile[pl.ds(row, BLK), pl.ds(col, BLK)] = got[slot]

        @pl.when(again == 1)
        def _():
            @pl.when(later == 0)
            def _():
                total[...] = got[code_ref[step - 1] & 255].astype(jnp.float32)

            value = total[...] + got[slot].astype(jnp.float32)
            total[...] = value
            tile[pl.ds(row, BLK), pl.ds(col, BLK)] = value.astype(tile.dtype)

        return carry

    lax.fori_loop(0, code_ref[slots], insert, 0)
    put_tile = pltpu.make_async_copy(tile, tile_hbm, sems.at[2])
    put_tile.start()
    get_omega.wait()
    sketch_ref[...] = jnp.zeros_like(sketch_ref)
    depth = 1024

    def multiply(step, carry):
        at = pl.ds(pl.multiple_of(step * depth, depth), depth)
        sketch_ref[...] += jnp.dot(tile[:, at], omega[at, :], preferred_element_type=jnp.float32)
        return carry

    lax.fori_loop(0, cols // depth, multiply, 0)
    put_tile.wait()


def tile_and_sketch(code, got, omega, rows, cols):
    slots, rank = got.shape[0], omega.shape[1]
    return pl.pallas_call(
        tile_kernel,
        grid_spec=pltpu.PrefetchScalarGridSpec(
            num_scalar_prefetch=1,
            grid=(),
            in_specs=[pl.BlockSpec(memory_space=pl.ANY)] * 2,
            out_specs=[
                pl.BlockSpec(memory_space=pl.ANY),
                pl.BlockSpec(memory_space=pltpu.VMEM),
            ],
            scratch_shapes=[
                pltpu.VMEM((slots, BLK, BLK), jnp.bfloat16),
                pltpu.VMEM((cols, rank), jnp.bfloat16),
                pltpu.VMEM((rows, cols), jnp.bfloat16),
                pltpu.VMEM((BLK, BLK), jnp.float32),
                pltpu.SemaphoreType.DMA((3,)),
            ],
        ),
        out_shape=[
            jax.ShapeDtypeStruct((rows, cols), jnp.bfloat16),
            jax.ShapeDtypeStruct((rows, rank), jnp.float32),
        ],
        compiler_params=pltpu.CompilerParams(vmem_limit_bytes=52 * MIB),
        cost_estimate=pl.CostEstimate(
            flops=2 * rows * cols * rank,
            bytes_accessed=2 * (got.size + omega.size + rows * cols),
            transcendentals=0,
        ),
        name="tile_and_sketch",
    )(code, got, omega)


def factor_kernel(scale, gram_ref, out_ref, work):
    n = gram_ref.shape[0]
    work[...] = gram_ref[...] * scale
    row = lax.broadcasted_iota(jnp.int32, (n, n), 0)
    lane = lax.broadcasted_iota(jnp.int32, (n, n), 1)
    out_ref[...] = jnp.where(row == lane, 1.0, 0.0)
    sub = lax.broadcasted_iota(jnp.int32, (8, BLK), 0)
    lane8 = lax.broadcasted_iota(jnp.int32, (8, BLK), 1)
    groups = BLK // 8

    def spread(value, j):
        return jnp.broadcast_to(value[:, j : j + 1], (8, BLK))

    def block(panel, carry):
        at = pl.ds(pl.multiple_of(panel * BLK, BLK), BLK)
        left = [work[pl.ds(pl.multiple_of(panel * BLK + 8 * g, 8), 8), at] for g in range(groups)]
        right = [jnp.where(lane8 == sub + 8 * g, 1.0, 0.0) for g in range(groups)]
        for g0 in range(groups):
            own = [spread(left[g0], 8 * g0 + k) for k in range(8)]
            factors, pivots_left, pivots_right = {}, [], []
            for k in range(8):
                inverse = 1.0 / own[k][k : k + 1, :]
                for later in range(k + 1, 8):
                    factors[k, later] = own[later][k : k + 1, :] * inverse
                    own[later] = own[later] - own[k] * factors[k, later]
                pivots_left.append(left[g0][k : k + 1, :] * inverse)
                pivots_right.append(right[g0][k : k + 1, :] * inverse)
                column = jnp.where(sub > k, own[k], 0.0)
                left[g0] = left[g0] - column * pivots_left[k]
                right[g0] = right[g0] - column * pivots_right[k]
            for g in range(g0 + 1, groups):
                below = [spread(left[g], 8 * g0 + k) for k in range(8)]
                for k in range(8):
                    for later in range(k + 1, 8):
                        below[later] = below[later] - below[k] * factors[k, later]
                    left[g] = left[g] - below[k] * pivots_left[k]
                    right[g] = right[g] - below[k] * pivots_right[k]
        halves = []
        for g in range(groups):
            pivot = jnp.sum(
                jnp.where(lane8 == sub + 8 * g, left[g], 0.0), axis=1, keepdims=True
            )
            halves.append(right[g] * (1.0 / jnp.sqrt(pivot)))
        inverse_block = jnp.concatenate(halves, axis=0)
        both = jnp.concatenate([work[at, :], out_ref[at, :]], axis=1)
        upper = jnp.dot(inverse_block, both, precision=HIGHEST, preferred_element_type=jnp.float32)

        @pl.when(panel < n // BLK - 1)
        def _():
            lanes = lax.broadcasted_iota(jnp.int32, (BLK, n), 1)
            later = jnp.where(lanes >= (panel + 1) * BLK, upper[:, :n], 0.0)
            change = lax.dot_general(
                later, upper, (((0,), (0,)), ((), ())), precision=HIGHEST, preferred_element_type=jnp.float32
            )
            work[...] -= change[:, :n]
            out_ref[...] -= change[:, n:]

        out_ref[at, :] = upper[:, n:]
        return carry

    lax.fori_loop(0, n // BLK, block, 0)


def inverse_factor(gram, scale):
    n = gram.shape[0]
    return pl.pallas_call(
        functools.partial(factor_kernel, scale),
        in_specs=[pl.BlockSpec(memory_space=pltpu.VMEM)],
        out_specs=pl.BlockSpec(memory_space=pltpu.VMEM),
        out_shape=jax.ShapeDtypeStruct((n, n), jnp.float32),
        scratch_shapes=[pltpu.VMEM((n, n), jnp.float32)],
        compiler_params=pltpu.CompilerParams(vmem_limit_bytes=24 * MIB),
        cost_estimate=pl.CostEstimate(
            flops=1 << 35, bytes_accessed=2 * n * n * 4, transcendentals=0
        ),
        name="inverse_factor",
    )(gram)


def product_kernel(left_ref, own_ref, other_ref, out_ref):
    rows = own_ref.shape[0]
    total = jnp.dot(left_ref[:, :rows], own_ref[...], preferred_element_type=jnp.float32)
    total += jnp.dot(left_ref[:, rows:], other_ref[...], preferred_element_type=jnp.float32)
    out_ref[...] = total.astype(out_ref.dtype)


def product(left, own, other, width):
    rows, cols = own.shape
    half = left.shape[0]
    spec = pl.BlockSpec((rows, width), lambda k: (0, k))
    return pl.pallas_call(
        product_kernel,
        grid=(cols // width,),
        in_specs=[pl.BlockSpec((half, 2 * rows), lambda k: (0, 0)), spec, spec],
        out_specs=pl.BlockSpec((half, width), lambda k: (0, k)),
        out_shape=jax.ShapeDtypeStruct((half, cols), jnp.bfloat16),
        compiler_params=pltpu.CompilerParams(vmem_limit_bytes=56 * MIB),
        cost_estimate=pl.CostEstimate(
            flops=2 * half * 2 * rows * cols,
            bytes_accessed=4 * rows * cols + 2 * half * cols,
            transcendentals=0,
        ),
        name="product",
    )(left, own, other)


def on_device(blocks, owner, block_pos, omega):
    slot_count = blocks.shape[0]
    rank = omega.shape[1]
    row_devices = lax.axis_size("rows")
    col_devices = lax.axis_size("cols")
    devices_all = row_devices * col_devices
    everywhere = ("rows", "cols")
    capacity = max(2, 2 * slot_count // devices_all)
    slots = devices_all * capacity
    panel, cols = PBR * BLK, TBC * BLK
    total_rows = panel * row_devices
    core = lax.axis_index("rows") % 2
    swap = [(i, i ^ 1) for i in range(row_devices)]

    target = owner[:, 0]
    numbers = jnp.arange(slot_count, dtype=jnp.int32)
    same = (target[:, None] == target[None, :]) & (numbers[None, :] < numbers[:, None])
    place = target * capacity + jnp.sum(same.astype(jnp.int32), axis=1)
    spots = jnp.arange(slots, dtype=jnp.int32)
    hit = place[None, :] == spots[:, None]
    send_where = jnp.sum(jnp.where(hit, block_pos[None, :] + 1, 0), axis=1)
    send_blocks = bucket(place, blocks, slots)
    got_blocks = lax.all_to_all(
        send_blocks.reshape(devices_all, capacity, BLK, BLK), everywhere, 0, 0, tiled=True
    ).reshape(slots, BLK, BLK)
    got_where = lax.all_to_all(
        send_where.reshape(devices_all, capacity), everywhere, 0, 0, tiled=True
    ).reshape(slots)

    key = jnp.where(got_where == 0, PBR * TBC, got_where - 1)
    before = (key[None, :] < key[:, None]) | (
        (key[None, :] == key[:, None]) & (spots[None, :] < spots[:, None])
    )
    order = jnp.sum(before.astype(jnp.int32), axis=1)
    packed = key * slots + spots
    ordered = jnp.sum(jnp.where(order[None, :] == spots[:, None], packed[None, :], 0), axis=1)
    slot, where = ordered % slots, ordered // slots
    again = jnp.concatenate([jnp.zeros((1,), jnp.int32), (where[1:] == where[:-1]).astype(jnp.int32)])
    later = jnp.concatenate([jnp.zeros((1,), jnp.int32), again[:-1]])
    code = slot + (where // TBC) * 256 + (where % TBC) * 1024 + (again << 17) + (later << 18)
    filled = jnp.sum((key < PBR * TBC).astype(jnp.int32))
    code = jnp.concatenate([code, filled[None]])

    tile, part = tile_and_sketch(code, got_blocks, omega, panel, cols)
    other_tile = lax.ppermute(tile, "rows", swap)

    share = panel // col_devices
    parts = lax.all_to_all(part.reshape(col_devices, share, rank), "cols", 0, 0, tiled=True)
    own_share = jnp.sum(parts, axis=0)
    local_gram = lax.dot_general(
        own_share, own_share, (((0,), (0,)), ((), ())), precision=HIGHEST, preferred_element_type=jnp.float32
    )
    grams = lax.all_to_all(
        local_gram.reshape(devices_all, rank // devices_all, rank), everywhere, 0, 0, tiled=True
    )
    gram_rows, late_share = lax.optimization_barrier((jnp.sum(grams, axis=0), own_share))
    gram = lax.all_to_all(
        jnp.broadcast_to(gram_rows[None], (devices_all,) + gram_rows.shape), everywhere, 0, 0, tiled=True
    ).reshape(rank, rank)
    shares = [late_share] + [
        lax.ppermute(late_share, "cols", [(i, (i + d) % col_devices) for i in range(col_devices)])
        for d in range(1, col_devices)
    ]
    back = jnp.stack(shares[::-1] * 2)
    start = col_devices - 1 - lax.axis_index("cols")
    sketch = lax.dynamic_slice_in_dim(back, start, col_devices, 0).reshape(panel, rank)
    other_sketch = lax.ppermute(sketch, "rows", swap)
    inverse = inverse_factor(gram, 1.0 / total_rows)

    ranks = rank // row_devices
    half = rank // 2
    chips = row_devices // 2
    both = jnp.concatenate([sketch, other_sketch], axis=0)
    my_ranks = lax.dynamic_index_in_dim(
        inverse.reshape(chips, 2, ranks, rank), core, 1, keepdims=False
    ).reshape(half, rank)
    left = lax.dot_general(
        my_ranks, both, (((1,), (1,)), ((), ())), precision=HIGHEST, preferred_element_type=jnp.float32
    ).astype(jnp.bfloat16)

    slice_width = rank // col_devices
    my_rows = lax.dynamic_slice_in_dim(inverse, lax.axis_index("cols") * slice_width, slice_width, 0)
    basis = lax.dot_general(
        sketch, my_rows, (((1,), (1,)), ((), ())), precision=HIGHEST, preferred_element_type=jnp.float32
    ).astype(jnp.bfloat16)

    groups = [[2 * i + c for i in range(chips)] for c in range(2)]
    scaling = 1.0 / math.sqrt(total_rows)
    terms = product(left, tile, other_tile, cols // 4).reshape(chips, ranks, cols)
    terms, basis = lax.optimization_barrier((terms, basis))
    terms = lax.all_to_all(terms, "rows", 0, 0, axis_index_groups=groups, tiled=True)
    coefficients = jnp.sum(terms.astype(jnp.float32), axis=0) * scaling

    return basis, coefficients


def solution(mesh):
    in_specs = (
        P(("rows", "cols"), None, None),
        P(("rows", "cols"), None),
        P(("rows", "cols")),
        P("cols", None),
    )
    out_specs = (P("rows", "cols"), P("rows", "cols"))
    return jax.shard_map(
        on_device, mesh=mesh, in_specs=in_specs, out_specs=out_specs, check_vma=False
    )
```

```python
import functools
import math

import jax
import jax.numpy as jnp
from jax import lax
from jax.experimental import pallas as pl
from jax.experimental.pallas import tpu as pltpu
from jax.sharding import PartitionSpec as P

PBR = 4
TBC = 104
BLK = 128
HIGHEST = lax.Precision.HIGHEST
MIB = 1 << 20


def bucket_kernel(place_ref, blocks_ref, out_ref, sem):
    count = blocks_ref.shape[0]

    def issue(slot, carry):
        pltpu.make_async_copy(blocks_ref.at[slot], out_ref.at[place_ref[slot]], sem).start()
        return carry

    lax.fori_loop(0, count, issue, 0)
    pltpu.make_async_copy(blocks_ref, out_ref.at[pl.ds(0, count)], sem).wait()


def bucket(place, blocks, slots):
    return pl.pallas_call(
        bucket_kernel,
        grid_spec=pltpu.PrefetchScalarGridSpec(
            num_scalar_prefetch=1,
            grid=(),
            in_specs=[pl.BlockSpec(memory_space=pltpu.VMEM)],
            out_specs=pl.BlockSpec(memory_space=pl.ANY),
            scratch_shapes=[pltpu.SemaphoreType.DMA],
        ),
        out_shape=jax.ShapeDtypeStruct((slots,) + blocks.shape[1:], blocks.dtype),
        compiler_params=pltpu.CompilerParams(vmem_limit_bytes=56 * MIB),
        cost_estimate=pl.CostEstimate(flops=0, bytes_accessed=2 * blocks.size * 2, transcendentals=0),
        name="bucket",
    )(place, blocks)


def tile_kernel(code_ref, got_hbm, omega_hbm, tile_hbm, sketch_ref, got, omega, tile, total, sems):
    slots = got.shape[0]
    rows, cols = tile.shape
    get_blocks = pltpu.make_async_copy(got_hbm, got, sems.at[0])
    get_omega = pltpu.make_async_copy(omega_hbm, omega, sems.at[1])
    get_blocks.start()
    get_omega.start()

    def clear(step, carry):
        tile[pl.ds(pl.multiple_of(step * 16, 16), 16), :] = jnp.zeros((16, cols), tile.dtype)
        return carry

    lax.fori_loop(0, rows // 16, clear, 0)
    get_blocks.wait()

    def insert(step, carry):
        code = code_ref[step]
        slot = code & 255
        row = pl.multiple_of(((code >> 8) & 3) * BLK, BLK)
        col = pl.multiple_of(((code >> 10) & 127) * BLK, BLK)
        again = (code >> 17) & 1
        later = (code >> 18) & 1

        @pl.when(again == 0)
        def _():
            tile[pl.ds(row, BLK), pl.ds(col, BLK)] = got[slot]

        @pl.when(again == 1)
        def _():
            @pl.when(later == 0)
            def _():
                total[...] = got[code_ref[step - 1] & 255].astype(jnp.float32)

            value = total[...] + got[slot].astype(jnp.float32)
            total[...] = value
            tile[pl.ds(row, BLK), pl.ds(col, BLK)] = value.astype(tile.dtype)

        return carry

    lax.fori_loop(0, code_ref[slots], insert, 0)
    put_tile = pltpu.make_async_copy(tile, tile_hbm, sems.at[2])
    put_tile.start()
    get_omega.wait()
    sketch_ref[...] = jnp.zeros_like(sketch_ref)
    depth = 1024

    def multiply(step, carry):
        at = pl.ds(pl.multiple_of(step * depth, depth), depth)
        sketch_ref[...] += jnp.dot(tile[:, at], omega[at, :], preferred_element_type=jnp.float32)
        return carry

    lax.fori_loop(0, cols // depth, multiply, 0)
    put_tile.wait()


def tile_and_sketch(code, got, omega, rows, cols):
    slots, rank = got.shape[0], omega.shape[1]
    return pl.pallas_call(
        tile_kernel,
        grid_spec=pltpu.PrefetchScalarGridSpec(
            num_scalar_prefetch=1,
            grid=(),
            in_specs=[pl.BlockSpec(memory_space=pl.ANY)] * 2,
            out_specs=[
                pl.BlockSpec(memory_space=pl.ANY),
                pl.BlockSpec(memory_space=pltpu.VMEM),
            ],
            scratch_shapes=[
                pltpu.VMEM((slots, BLK, BLK), jnp.bfloat16),
                pltpu.VMEM((cols, rank), jnp.bfloat16),
                pltpu.VMEM((rows, cols), jnp.bfloat16),
                pltpu.VMEM((BLK, BLK), jnp.float32),
                pltpu.SemaphoreType.DMA((3,)),
            ],
        ),
        out_shape=[
            jax.ShapeDtypeStruct((rows, cols), jnp.bfloat16),
            jax.ShapeDtypeStruct((rows, rank), jnp.float32),
        ],
        compiler_params=pltpu.CompilerParams(vmem_limit_bytes=52 * MIB),
        cost_estimate=pl.CostEstimate(
            flops=2 * rows * cols * rank,
            bytes_accessed=2 * (got.size + omega.size + rows * cols),
            transcendentals=0,
        ),
        name="tile_and_sketch",
    )(code, got, omega)


def factor_kernel(scale, gram_ref, out_ref, work):
    n = gram_ref.shape[0]
    work[...] = gram_ref[...] * scale
    row = lax.broadcasted_iota(jnp.int32, (n, n), 0)
    lane = lax.broadcasted_iota(jnp.int32, (n, n), 1)
    out_ref[...] = jnp.where(row == lane, 1.0, 0.0)
    sub = lax.broadcasted_iota(jnp.int32, (8, BLK), 0)
    lane8 = lax.broadcasted_iota(jnp.int32, (8, BLK), 1)
    groups = BLK // 8

    def spread(value, j):
        return jnp.broadcast_to(value[:, j : j + 1], (8, BLK))

    def block(panel, carry):
        at = pl.ds(pl.multiple_of(panel * BLK, BLK), BLK)
        left = [work[pl.ds(pl.multiple_of(panel * BLK + 8 * g, 8), 8), at] for g in range(groups)]
        right = [jnp.where(lane8 == sub + 8 * g, 1.0, 0.0) for g in range(groups)]
        for g0 in range(groups):
            own = [spread(left[g0], 8 * g0 + k) for k in range(8)]
            factors, pivots_left, pivots_right = {}, [], []
            for k in range(8):
                inverse = 1.0 / own[k][k : k + 1, :]
                for later in range(k + 1, 8):
                    factors[k, later] = own[later][k : k + 1, :] * inverse
                    own[later] = own[later] - own[k] * factors[k, later]
                pivots_left.append(left[g0][k : k + 1, :] * inverse)
                pivots_right.append(right[g0][k : k + 1, :] * inverse)
                column = jnp.where(sub > k, own[k], 0.0)
                left[g0] = left[g0] - column * pivots_left[k]
                right[g0] = right[g0] - column * pivots_right[k]
            for g in range(g0 + 1, groups):
                below = [spread(left[g], 8 * g0 + k) for k in range(8)]
                for k in range(8):
                    for later in range(k + 1, 8):
                        below[later] = below[later] - below[k] * factors[k, later]
                    left[g] = left[g] - below[k] * pivots_left[k]
                    right[g] = right[g] - below[k] * pivots_right[k]
        halves = []
        for g in range(groups):
            pivot = jnp.sum(
                jnp.where(lane8 == sub + 8 * g, left[g], 0.0), axis=1, keepdims=True
            )
            halves.append(right[g] * (1.0 / jnp.sqrt(pivot)))
        inverse_block = jnp.concatenate(halves, axis=0)
        both = jnp.concatenate([work[at, :], out_ref[at, :]], axis=1)
        upper = jnp.dot(inverse_block, both, precision=HIGHEST, preferred_element_type=jnp.float32)

        @pl.when(panel < n // BLK - 1)
        def _():
            lanes = lax.broadcasted_iota(jnp.int32, (BLK, n), 1)
            later = jnp.where(lanes >= (panel + 1) * BLK, upper[:, :n], 0.0)
            change = lax.dot_general(
                later, upper, (((0,), (0,)), ((), ())), precision=HIGHEST, preferred_element_type=jnp.float32
            )
            work[...] -= change[:, :n]
            out_ref[...] -= change[:, n:]

        out_ref[at, :] = upper[:, n:]
        return carry

    lax.fori_loop(0, n // BLK, block, 0)


def inverse_factor(gram, scale):
    n = gram.shape[0]
    return pl.pallas_call(
        functools.partial(factor_kernel, scale),
        in_specs=[pl.BlockSpec(memory_space=pltpu.VMEM)],
        out_specs=pl.BlockSpec(memory_space=pltpu.VMEM),
        out_shape=jax.ShapeDtypeStruct((n, n), jnp.float32),
        scratch_shapes=[pltpu.VMEM((n, n), jnp.float32)],
        compiler_params=pltpu.CompilerParams(vmem_limit_bytes=24 * MIB),
        cost_estimate=pl.CostEstimate(
            flops=1 << 35, bytes_accessed=2 * n * n * 4, transcendentals=0
        ),
        name="inverse_factor",
    )(gram)


FAR = 2
FORWARD = ((2, 0), (2, 1)) + tuple((1, e) for e in range(4))
BACKWARD = ((2, 2), (2, 3)) + tuple((3, e) for e in range(4))
STAY = tuple((0, e) for e in range(4))
PIECES = FORWARD + BACKWARD + STAY


def basis_kernel(at_ref, inverse_ref, own_ref, other_ref, left_ref, turned_ref, basis_ref, chosen):
    pieces = len(PIECES)
    size = chosen.shape[0] // pieces
    panel = own_ref.shape[0]
    for k in range(pieces):
        chosen[k * size : (k + 1) * size, :] = inverse_ref[
            pl.ds(pl.multiple_of(at_ref[k], size), size), :
        ]
    contract = (((1,), (1,)), ((), ()))
    for i, sketch_ref in enumerate((own_ref, other_ref)):
        left = lax.dot_general(
            chosen[...], sketch_ref[...], contract, precision=HIGHEST, preferred_element_type=jnp.float32
        ).astype(left_ref.dtype)
        left_ref[:, i * panel : (i + 1) * panel] = left
        turned_ref[:, i * panel : (i + 1) * panel] = jnp.concatenate(
            [left[PIECES.index((b, a)) * size :][:size] for a, b in PIECES], axis=0
        )
    width = basis_ref.shape[1]
    basis_ref[...] = lax.dot_general(
        own_ref[...],
        inverse_ref[pl.ds(pl.multiple_of(at_ref[pieces], width), width), :],
        contract,
        precision=HIGHEST,
        preferred_element_type=jnp.float32,
    ).astype(basis_ref.dtype)


def basis_parts(at, inverse, own, other, half, width):
    panel, rank = own.shape
    whole = pl.BlockSpec(memory_space=pltpu.VMEM)
    return pl.pallas_call(
        basis_kernel,
        grid_spec=pltpu.PrefetchScalarGridSpec(
            num_scalar_prefetch=1,
            grid=(),
            in_specs=[whole] * 3,
            out_specs=[whole] * 3,
            scratch_shapes=[pltpu.VMEM((half, rank), jnp.float32)],
        ),
        out_shape=[
            jax.ShapeDtypeStruct((half, 2 * panel), jnp.bfloat16),
            jax.ShapeDtypeStruct((half, 2 * panel), jnp.bfloat16),
            jax.ShapeDtypeStruct((panel, width), jnp.bfloat16),
        ],
        compiler_params=pltpu.CompilerParams(vmem_limit_bytes=32 * MIB),
        cost_estimate=pl.CostEstimate(
            flops=12 * rank * panel * (2 * half + width), bytes_accessed=6 * rank * panel, transcendentals=0
        ),
        name="basis_parts",
    )(at, inverse, own, other)


def product_kernel(scale, left_ref, own_ref, other_ref, *out_refs):
    rows = own_ref.shape[0]
    total = jnp.dot(left_ref[:, :rows], own_ref[...], preferred_element_type=jnp.float32)
    total += jnp.dot(left_ref[:, rows:], other_ref[...], preferred_element_type=jnp.float32)
    total *= scale
    start = 0
    for out_ref in out_refs:
        end = start + out_ref.shape[0]
        out_ref[...] = total[start:end].astype(out_ref.dtype)
        start = end


def product(left, own, other, part, parts, width, scale):
    rows, cols = own.shape
    half = left.shape[0]
    steps = cols // parts // width
    size = half // len(PIECES)
    heights = [size * len(g) for g in (FORWARD, BACKWARD, STAY)]
    spec = pl.BlockSpec((rows, width), lambda k: (0, part * steps + k))
    return pl.pallas_call(
        functools.partial(product_kernel, scale),
        grid=(steps,),
        in_specs=[pl.BlockSpec((half, 2 * rows), lambda k: (0, 0)), spec, spec],
        out_specs=[pl.BlockSpec((height, width), lambda k: (0, k)) for height in heights],
        out_shape=[
            jax.ShapeDtypeStruct((height, cols // parts), jnp.float32 if i == 2 else jnp.bfloat16)
            for i, height in enumerate(heights)
        ],
        compiler_params=pltpu.CompilerParams(vmem_limit_bytes=40 * MIB),
        cost_estimate=pl.CostEstimate(
            flops=4 * half * rows * cols // parts,
            bytes_accessed=(4 * rows * cols + 2 * half * cols) // parts,
            transcendentals=0,
        ),
        name="product",
    )(left, own, other)


def on_device(blocks, owner, block_pos, omega):
    slot_count = blocks.shape[0]
    rank = omega.shape[1]
    row_devices = lax.axis_size("rows")
    col_devices = lax.axis_size("cols")
    devices_all = row_devices * col_devices
    everywhere = ("rows", "cols")
    capacity = max(2, 2 * slot_count // devices_all)
    slots = devices_all * capacity
    panel, cols = PBR * BLK, TBC * BLK
    total_rows = panel * row_devices
    core = lax.axis_index("rows") % 2
    swap = [(i, i ^ 1) for i in range(row_devices)]

    target = owner[:, 0]
    numbers = jnp.arange(slot_count, dtype=jnp.int32)
    same = (target[:, None] == target[None, :]) & (numbers[None, :] < numbers[:, None])
    place = target * capacity + jnp.sum(same.astype(jnp.int32), axis=1)
    spots = jnp.arange(slots, dtype=jnp.int32)
    hit = place[None, :] == spots[:, None]
    send_where = jnp.sum(jnp.where(hit, block_pos[None, :] + 1, 0), axis=1)
    send_blocks = bucket(place, blocks, slots)
    got_blocks = lax.all_to_all(
        send_blocks.reshape(devices_all, capacity, BLK, BLK), everywhere, 0, 0, tiled=True
    ).reshape(slots, BLK, BLK)
    got_where = lax.all_to_all(
        send_where.reshape(devices_all, capacity), everywhere, 0, 0, tiled=True
    ).reshape(slots)

    key = jnp.where(got_where == 0, PBR * TBC, got_where - 1)
    before = (key[None, :] < key[:, None]) | (
        (key[None, :] == key[:, None]) & (spots[None, :] < spots[:, None])
    )
    order = jnp.sum(before.astype(jnp.int32), axis=1)
    packed = key * slots + spots
    ordered = jnp.sum(jnp.where(order[None, :] == spots[:, None], packed[None, :], 0), axis=1)
    slot, where = ordered % slots, ordered // slots
    again = jnp.concatenate([jnp.zeros((1,), jnp.int32), (where[1:] == where[:-1]).astype(jnp.int32)])
    later = jnp.concatenate([jnp.zeros((1,), jnp.int32), again[:-1]])
    code = slot + (where // TBC) * 256 + (where % TBC) * 1024 + (again << 17) + (later << 18)
    filled = jnp.sum((key < PBR * TBC).astype(jnp.int32))
    code = jnp.concatenate([code, filled[None]])

    tile, part = tile_and_sketch(code, got_blocks, omega, panel, cols)
    other_tile = lax.ppermute(tile, "rows", swap)

    share = panel // col_devices
    parts = lax.all_to_all(part.reshape(col_devices, share, rank), "cols", 0, 0, tiled=True)
    own_share = jnp.sum(parts, axis=0)
    local_gram = lax.dot_general(
        own_share, own_share, (((0,), (0,)), ((), ())), precision=HIGHEST, preferred_element_type=jnp.float32
    )
    grams = lax.all_to_all(
        local_gram.reshape(devices_all, rank // devices_all, rank), everywhere, 0, 0, tiled=True
    )
    gram_rows, late_share = lax.optimization_barrier((jnp.sum(grams, axis=0), own_share))
    gram = lax.all_to_all(
        jnp.broadcast_to(gram_rows[None], (devices_all,) + gram_rows.shape), everywhere, 0, 0, tiled=True
    ).reshape(rank, rank)
    shares = [late_share] + [
        lax.ppermute(late_share, "cols", [(i, (i + d) % col_devices) for i in range(col_devices)])
        for d in range(1, col_devices)
    ]
    back = jnp.stack(shares[::-1] * 2)
    start = col_devices - 1 - lax.axis_index("cols")
    sketch = lax.dynamic_slice_in_dim(back, start, col_devices, 0).reshape(panel, rank)
    other_sketch = lax.ppermute(sketch, "rows", swap)
    inverse = inverse_factor(gram, 1.0 / total_rows)

    ranks = rank // row_devices
    chips = row_devices // 2
    along = math.isqrt(chips)
    chip = lax.axis_index("rows") // 2
    x, y = chip // along, chip % along
    at = [(((x + a) % along * along + (y + b) % along) * 2 + core) * ranks for a, b in PIECES]
    width = rank // col_devices
    at.append(lax.axis_index("cols") * width)
    left, turned, basis = basis_parts(
        jnp.stack(at).astype(jnp.int32), inverse, sketch, other_sketch, rank // 2, width
    )

    def shift(over_x, steps):
        moves = []
        for i in range(row_devices):
            a, b = i // 2 // along, i // 2 % along
            a, b = ((a + steps) % along, b) if over_x else (a, (b + steps) % along)
            moves.append((i, (a * along + b) * 2 + i % 2))
        return functools.partial(lax.ppermute, axis_name="rows", perm=moves)

    def scatter(part, factor, x_first):
        ahead, behind, total = product(
            factor, tile, other_tile, part, 2, cols // 4, 1.0 / math.sqrt(total_rows)
        )
        forward, backward = shift(x_first, 1), shift(x_first, -1)
        ahead, behind = forward(ahead), backward(behind)
        far, back_far = forward(ahead[: FAR * ranks]), backward(behind[: FAR * ranks])
        total += ahead[FAR * ranks :].astype(jnp.float32) + behind[FAR * ranks :].astype(jnp.float32)
        total += jnp.concatenate([far, back_far], axis=0).astype(jnp.float32)
        terms = [total[i * ranks : (i + 1) * ranks] for i in range(along)]
        result = terms[0]
        for i in range(1, along):
            result += shift(not x_first, i)(terms[i].astype(jnp.bfloat16)).astype(jnp.float32)
        return result

    coefficients = jnp.concatenate([scatter(0, left, True), scatter(1, turned, False)], axis=1)
    return basis, coefficients


def solution(mesh):
    in_specs = (
        P(("rows", "cols"), None, None),
        P(("rows", "cols"), None),
        P(("rows", "cols")),
        P("cols", None),
    )
    out_specs = (P("rows", "cols"), P("rows", "cols"))
    return jax.shard_map(
        on_device, mesh=mesh, in_specs=in_specs, out_specs=out_specs, check_vma=False
    )
```

```python
import functools
import math

import jax
import jax.numpy as jnp
from jax import lax
from jax.experimental import pallas as pl
from jax.experimental.pallas import tpu as pltpu
from jax.sharding import PartitionSpec as P

PBR = 4
TBC = 104
BLK = 128
HIGHEST = lax.Precision.HIGHEST
MIB = 1 << 20


def bucket_kernel(place_ref, blocks_ref, out_ref, sem):
    count = blocks_ref.shape[0]

    def issue(slot, carry):
        pltpu.make_async_copy(blocks_ref.at[slot], out_ref.at[place_ref[slot]], sem).start()
        return carry

    lax.fori_loop(0, count, issue, 0)
    pltpu.make_async_copy(blocks_ref, out_ref.at[pl.ds(0, count)], sem).wait()


def bucket(place, blocks, slots):
    return pl.pallas_call(
        bucket_kernel,
        grid_spec=pltpu.PrefetchScalarGridSpec(
            num_scalar_prefetch=1,
            grid=(),
            in_specs=[pl.BlockSpec(memory_space=pltpu.VMEM)],
            out_specs=pl.BlockSpec(memory_space=pl.ANY),
            scratch_shapes=[pltpu.SemaphoreType.DMA],
        ),
        out_shape=jax.ShapeDtypeStruct((slots,) + blocks.shape[1:], blocks.dtype),
        compiler_params=pltpu.CompilerParams(vmem_limit_bytes=56 * MIB),
        cost_estimate=pl.CostEstimate(flops=0, bytes_accessed=2 * blocks.size * 2, transcendentals=0),
        name="bucket",
    )(place, blocks)


def tile_kernel(code_ref, got_hbm, omega_hbm, tile_hbm, sketch_ref, got, omega, tile, total, sems):
    slots = got.shape[0]
    rows, cols = tile.shape
    get_blocks = pltpu.make_async_copy(got_hbm, got, sems.at[0])
    get_omega = pltpu.make_async_copy(omega_hbm, omega, sems.at[1])
    get_blocks.start()
    get_omega.start()

    def clear(step, carry):
        tile[pl.ds(pl.multiple_of(step * 16, 16), 16), :] = jnp.zeros((16, cols), tile.dtype)
        return carry

    lax.fori_loop(0, rows // 16, clear, 0)
    get_blocks.wait()

    def insert(step, carry):
        code = code_ref[step]
        slot = code & 255
        row = pl.multiple_of(((code >> 8) & 3) * BLK, BLK)
        col = pl.multiple_of(((code >> 10) & 127) * BLK, BLK)
        again = (code >> 17) & 1
        later = (code >> 18) & 1

        @pl.when(again == 0)
        def _():
            tile[pl.ds(row, BLK), pl.ds(col, BLK)] = got[slot]

        @pl.when(again == 1)
        def _():
            @pl.when(later == 0)
            def _():
                total[...] = got[code_ref[step - 1] & 255].astype(jnp.float32)

            value = total[...] + got[slot].astype(jnp.float32)
            total[...] = value
            tile[pl.ds(row, BLK), pl.ds(col, BLK)] = value.astype(tile.dtype)

        return carry

    lax.fori_loop(0, code_ref[slots], insert, 0)
    put_tile = pltpu.make_async_copy(tile, tile_hbm, sems.at[2])
    put_tile.start()
    get_omega.wait()
    sketch_ref[...] = jnp.zeros_like(sketch_ref)
    depth = 1024

    def multiply(step, carry):
        at = pl.ds(pl.multiple_of(step * depth, depth), depth)
        sketch_ref[...] += jnp.dot(tile[:, at], omega[at, :], preferred_element_type=jnp.float32)
        return carry

    lax.fori_loop(0, cols // depth, multiply, 0)
    put_tile.wait()


def tile_and_sketch(code, got, omega, rows, cols):
    slots, rank = got.shape[0], omega.shape[1]
    return pl.pallas_call(
        tile_kernel,
        grid_spec=pltpu.PrefetchScalarGridSpec(
            num_scalar_prefetch=1,
            grid=(),
            in_specs=[pl.BlockSpec(memory_space=pl.ANY)] * 2,
            out_specs=[
                pl.BlockSpec(memory_space=pl.ANY),
                pl.BlockSpec(memory_space=pltpu.VMEM),
            ],
            scratch_shapes=[
                pltpu.VMEM((slots, BLK, BLK), jnp.bfloat16),
                pltpu.VMEM((cols, rank), jnp.bfloat16),
                pltpu.VMEM((rows, cols), jnp.bfloat16),
                pltpu.VMEM((BLK, BLK), jnp.float32),
                pltpu.SemaphoreType.DMA((3,)),
            ],
        ),
        out_shape=[
            jax.ShapeDtypeStruct((rows, cols), jnp.bfloat16),
            jax.ShapeDtypeStruct((rows, rank), jnp.float32),
        ],
        compiler_params=pltpu.CompilerParams(vmem_limit_bytes=52 * MIB),
        cost_estimate=pl.CostEstimate(
            flops=2 * rows * cols * rank,
            bytes_accessed=2 * (got.size + omega.size + rows * cols),
            transcendentals=0,
        ),
        name="tile_and_sketch",
    )(code, got, omega)


def upper_rows(n):
    start = 0
    for at in range(0, n, BLK):
        yield at, start, n - at
        start += n - at


def gram_kernel(parts_ref, share_ref, packed_ref):
    share = parts_ref[0]
    for i in range(1, parts_ref.shape[0]):
        share += parts_ref[i]
    share_ref[...] = share
    for at, start, width in upper_rows(share.shape[1]):
        packed_ref[:, start : start + width] = lax.dot_general(
            share[:, at : at + BLK],
            share[:, at:],
            (((0,), (0,)), ((), ())),
            precision=HIGHEST,
            preferred_element_type=jnp.float32,
        )


def share_and_gram(parts):
    _, share, rank = parts.shape
    packed = sum(width for _, _, width in upper_rows(rank))
    whole = pl.BlockSpec(memory_space=pltpu.VMEM)
    return pl.pallas_call(
        gram_kernel,
        in_specs=[whole],
        out_specs=[whole] * 2,
        out_shape=[
            jax.ShapeDtypeStruct((share, rank), jnp.float32),
            jax.ShapeDtypeStruct((BLK, packed), jnp.float32),
        ],
        compiler_params=pltpu.CompilerParams(vmem_limit_bytes=24 * MIB),
        cost_estimate=pl.CostEstimate(
            flops=12 * share * rank * rank, bytes_accessed=8 * parts.size, transcendentals=0
        ),
        name="share_and_gram",
    )(parts)


def factor_kernel(scale, gram_ref, out_ref, work):
    n = work.shape[0]
    work[...] = jnp.zeros_like(work)
    for at, start, width in upper_rows(n):
        work[at : at + BLK, at:] = gram_ref[:, start : start + width] * scale
    row = lax.broadcasted_iota(jnp.int32, (n, n), 0)
    lane = lax.broadcasted_iota(jnp.int32, (n, n), 1)
    out_ref[...] = jnp.where(row == lane, 1.0, 0.0)
    sub = lax.broadcasted_iota(jnp.int32, (8, BLK), 0)
    lane8 = lax.broadcasted_iota(jnp.int32, (8, BLK), 1)
    groups = BLK // 8

    def spread(value, j):
        return jnp.broadcast_to(value[:, j : j + 1], (8, BLK))

    def block(panel, carry):
        at = pl.ds(pl.multiple_of(panel * BLK, BLK), BLK)
        left = [work[pl.ds(pl.multiple_of(panel * BLK + 8 * g, 8), 8), at] for g in range(groups)]
        right = [jnp.where(lane8 == sub + 8 * g, 1.0, 0.0) for g in range(groups)]
        for g0 in range(groups):
            own = [spread(left[g0], 8 * g0 + k) for k in range(8)]
            factors, pivots_left, pivots_right = {}, [], []
            for k in range(8):
                inverse = 1.0 / own[k][k : k + 1, :]
                for later in range(k + 1, 8):
                    factors[k, later] = own[later][k : k + 1, :] * inverse
                    own[later] = own[later] - own[k] * factors[k, later]
                pivots_left.append(left[g0][k : k + 1, :] * inverse)
                pivots_right.append(right[g0][k : k + 1, :] * inverse)
                column = jnp.where(sub > k, own[k], 0.0)
                left[g0] = left[g0] - column * pivots_left[k]
                right[g0] = right[g0] - column * pivots_right[k]
            for g in range(g0 + 1, groups):
                below = [spread(left[g], 8 * g0 + k) for k in range(8)]
                for k in range(8):
                    for later in range(k + 1, 8):
                        below[later] = below[later] - below[k] * factors[k, later]
                    left[g] = left[g] - below[k] * pivots_left[k]
                    right[g] = right[g] - below[k] * pivots_right[k]
        halves = []
        for g in range(groups):
            pivot = jnp.sum(
                jnp.where(lane8 == sub + 8 * g, left[g], 0.0), axis=1, keepdims=True
            )
            halves.append(right[g] * (1.0 / jnp.sqrt(pivot)))
        inverse_block = jnp.concatenate(halves, axis=0)
        both = jnp.concatenate([work[at, :], out_ref[at, :]], axis=1)
        upper = jnp.dot(inverse_block, both, precision=HIGHEST, preferred_element_type=jnp.float32)

        @pl.when(panel < n // BLK - 1)
        def _():
            lanes = lax.broadcasted_iota(jnp.int32, (BLK, n), 1)
            later = jnp.where(lanes >= (panel + 1) * BLK, upper[:, :n], 0.0)
            change = lax.dot_general(
                later, upper, (((0,), (0,)), ((), ())), precision=HIGHEST, preferred_element_type=jnp.float32
            )
            work[...] -= change[:, :n]
            out_ref[...] -= change[:, n:]

        out_ref[at, :] = upper[:, n:]
        return carry

    lax.fori_loop(0, n // BLK, block, 0)


def inverse_factor(gram, n, scale):
    return pl.pallas_call(
        functools.partial(factor_kernel, scale),
        in_specs=[pl.BlockSpec(memory_space=pltpu.VMEM)],
        out_specs=pl.BlockSpec(memory_space=pltpu.VMEM),
        out_shape=jax.ShapeDtypeStruct((n, n), jnp.float32),
        scratch_shapes=[pltpu.VMEM((n, n), jnp.float32)],
        compiler_params=pltpu.CompilerParams(vmem_limit_bytes=24 * MIB),
        cost_estimate=pl.CostEstimate(
            flops=1 << 35, bytes_accessed=2 * n * n * 4, transcendentals=0
        ),
        name="inverse_factor",
    )(gram)


FAR = 2
FORWARD = ((2, 0), (2, 1)) + tuple((1, e) for e in range(4))
BACKWARD = ((2, 2), (2, 3)) + tuple((3, e) for e in range(4))
STAY = tuple((0, e) for e in range(4))
PIECES = FORWARD + BACKWARD + STAY


def basis_kernel(at_ref, inverse_ref, own_ref, other_ref, left_ref, turned_ref, basis_ref, chosen):
    pieces = len(PIECES)
    size = chosen.shape[0] // pieces
    panel = own_ref.shape[0]
    for k in range(pieces):
        chosen[k * size : (k + 1) * size, :] = inverse_ref[
            pl.ds(pl.multiple_of(at_ref[k], size), size), :
        ]
    contract = (((1,), (1,)), ((), ()))
    for i, sketch_ref in enumerate((own_ref, other_ref)):
        left = lax.dot_general(
            chosen[...], sketch_ref[...], contract, precision=HIGHEST, preferred_element_type=jnp.float32
        ).astype(left_ref.dtype)
        left_ref[:, i * panel : (i + 1) * panel] = left
        turned_ref[:, i * panel : (i + 1) * panel] = jnp.concatenate(
            [left[PIECES.index((b, a)) * size :][:size] for a, b in PIECES], axis=0
        )
    width = basis_ref.shape[1]
    basis_ref[...] = lax.dot_general(
        own_ref[...],
        inverse_ref[pl.ds(pl.multiple_of(at_ref[pieces], width), width), :],
        contract,
        precision=HIGHEST,
        preferred_element_type=jnp.float32,
    ).astype(basis_ref.dtype)


def basis_parts(at, inverse, own, other, half, width):
    panel, rank = own.shape
    whole = pl.BlockSpec(memory_space=pltpu.VMEM)
    return pl.pallas_call(
        basis_kernel,
        grid_spec=pltpu.PrefetchScalarGridSpec(
            num_scalar_prefetch=1,
            grid=(),
            in_specs=[whole] * 3,
            out_specs=[whole] * 3,
            scratch_shapes=[pltpu.VMEM((half, rank), jnp.float32)],
        ),
        out_shape=[
            jax.ShapeDtypeStruct((half, 2 * panel), jnp.bfloat16),
            jax.ShapeDtypeStruct((half, 2 * panel), jnp.bfloat16),
            jax.ShapeDtypeStruct((panel, width), jnp.bfloat16),
        ],
        compiler_params=pltpu.CompilerParams(vmem_limit_bytes=32 * MIB),
        cost_estimate=pl.CostEstimate(
            flops=12 * rank * panel * (2 * half + width), bytes_accessed=6 * rank * panel, transcendentals=0
        ),
        name="basis_parts",
    )(at, inverse, own, other)


def product_kernel(scale, left_ref, own_ref, other_ref, *out_refs):
    rows = own_ref.shape[0]
    total = jnp.dot(left_ref[:, :rows], own_ref[...], preferred_element_type=jnp.float32)
    total += jnp.dot(left_ref[:, rows:], other_ref[...], preferred_element_type=jnp.float32)
    total *= scale
    start = 0
    for out_ref in out_refs:
        end = start + out_ref.shape[0]
        out_ref[...] = total[start:end].astype(out_ref.dtype)
        start = end


def product(left, own, other, first, width, steps, scale):
    rows = own.shape[0]
    half = left.shape[0]
    count = width * steps
    size = half // len(PIECES)
    heights = [size * len(g) for g in (FORWARD, BACKWARD, STAY)]
    spec = pl.BlockSpec(
        (pl.Element(rows), pl.Element(width)), lambda k: (0, pl.multiple_of(first + k * width, BLK))
    )
    return pl.pallas_call(
        functools.partial(product_kernel, scale),
        grid=(steps,),
        in_specs=[pl.BlockSpec((half, 2 * rows), lambda k: (0, 0)), spec, spec],
        out_specs=[pl.BlockSpec((height, width), lambda k: (0, k)) for height in heights],
        out_shape=[
            jax.ShapeDtypeStruct((height, count), jnp.float32 if i == 2 else jnp.bfloat16)
            for i, height in enumerate(heights)
        ],
        compiler_params=pltpu.CompilerParams(vmem_limit_bytes=40 * MIB),
        cost_estimate=pl.CostEstimate(
            flops=4 * half * rows * count,
            bytes_accessed=(4 * rows + 2 * half) * count,
            transcendentals=0,
        ),
        name="product",
    )(left, own, other)


def on_device(blocks, owner, block_pos, omega):
    slot_count = blocks.shape[0]
    rank = omega.shape[1]
    row_devices = lax.axis_size("rows")
    col_devices = lax.axis_size("cols")
    devices_all = row_devices * col_devices
    everywhere = ("rows", "cols")
    capacity = max(2, 2 * slot_count // devices_all)
    slots = devices_all * capacity
    panel, cols = PBR * BLK, TBC * BLK
    total_rows = panel * row_devices
    core = lax.axis_index("rows") % 2
    swap = [(i, i ^ 1) for i in range(row_devices)]

    target = owner[:, 0]
    numbers = jnp.arange(slot_count, dtype=jnp.int32)
    same = (target[:, None] == target[None, :]) & (numbers[None, :] < numbers[:, None])
    place = target * capacity + jnp.sum(same.astype(jnp.int32), axis=1)
    spots = jnp.arange(slots, dtype=jnp.int32)
    hit = place[None, :] == spots[:, None]
    send_where = jnp.sum(jnp.where(hit, block_pos[None, :] + 1, 0), axis=1)
    send_blocks = bucket(place, blocks, slots)
    got_blocks = lax.all_to_all(
        send_blocks.reshape(devices_all, capacity, BLK, BLK), everywhere, 0, 0, tiled=True
    ).reshape(slots, BLK, BLK)
    got_where = lax.all_to_all(
        send_where.reshape(devices_all, capacity), everywhere, 0, 0, tiled=True
    ).reshape(slots)

    key = jnp.where(got_where == 0, PBR * TBC, got_where - 1)
    before = (key[None, :] < key[:, None]) | (
        (key[None, :] == key[:, None]) & (spots[None, :] < spots[:, None])
    )
    order = jnp.sum(before.astype(jnp.int32), axis=1)
    packed = key * slots + spots
    ordered = jnp.sum(jnp.where(order[None, :] == spots[:, None], packed[None, :], 0), axis=1)
    slot, where = ordered % slots, ordered // slots
    again = jnp.concatenate([jnp.zeros((1,), jnp.int32), (where[1:] == where[:-1]).astype(jnp.int32)])
    later = jnp.concatenate([jnp.zeros((1,), jnp.int32), again[:-1]])
    code = slot + (where // TBC) * 256 + (where % TBC) * 1024 + (again << 17) + (later << 18)
    filled = jnp.sum((key < PBR * TBC).astype(jnp.int32))
    code = jnp.concatenate([code, filled[None]])

    tile, part = tile_and_sketch(code, got_blocks, omega, panel, cols)
    other_tile = lax.ppermute(tile, "rows", swap)

    share = panel // col_devices
    parts = lax.all_to_all(part.reshape(col_devices, share, rank), "cols", 0, 0, tiled=True)
    own_share, local_gram = share_and_gram(parts)
    packed = local_gram.shape[1]
    gram_rows = (devices_all, BLK // devices_all, packed)
    grams = lax.all_to_all(local_gram.reshape(gram_rows), everywhere, 0, 0, tiled=True)
    gram, late_share = lax.optimization_barrier((jnp.sum(grams, axis=0), own_share))
    gram = lax.all_to_all(
        jnp.broadcast_to(gram[None], gram_rows), everywhere, 0, 0, tiled=True
    ).reshape(BLK, packed)
    shares = [late_share] + [
        lax.ppermute(late_share, "cols", [(i, (i + d) % col_devices) for i in range(col_devices)])
        for d in range(1, col_devices)
    ]
    back = jnp.stack(shares[::-1] * 2)
    start = col_devices - 1 - lax.axis_index("cols")
    sketch = lax.dynamic_slice_in_dim(back, start, col_devices, 0).reshape(panel, rank)
    other_sketch = lax.ppermute(sketch, "rows", swap)
    inverse = inverse_factor(gram, rank, 1.0 / total_rows)

    ranks = rank // row_devices
    chips = row_devices // 2
    along = math.isqrt(chips)
    chip = lax.axis_index("rows") // 2
    x, y = chip // along, chip % along
    at = [(((x + a) % along * along + (y + b) % along) * 2 + core) * ranks for a, b in PIECES]
    width = rank // col_devices
    at.append(lax.axis_index("cols") * width)
    left, turned, basis = basis_parts(
        jnp.stack(at).astype(jnp.int32), inverse, sketch, other_sketch, rank // 2, width
    )

    def shift(over_x, steps):
        moves = []
        for i in range(row_devices):
            a, b = i // 2 // along, i // 2 % along
            a, b = ((a + steps) % along, b) if over_x else (a, (b + steps) % along)
            moves.append((i, (a * along + b) * 2 + i % 2))
        return functools.partial(lax.ppermute, axis_name="rows", perm=moves)

    def scatter(first, count, factor, x_first):
        ahead, behind, total = product(
            factor, tile, other_tile, first, count // 2, 2, 1.0 / math.sqrt(total_rows)
        )
        forward, backward = shift(x_first, 1), shift(x_first, -1)
        ahead, behind = forward(ahead), backward(behind)
        far, back_far = forward(ahead[: FAR * ranks]), backward(behind[: FAR * ranks])
        total += ahead[FAR * ranks :].astype(jnp.float32) + behind[FAR * ranks :].astype(jnp.float32)
        total += jnp.concatenate([far, back_far], axis=0).astype(jnp.float32)
        terms = [total[i * ranks : (i + 1) * ranks] for i in range(along)]
        result = terms[0]
        for i in range(1, along):
            result += shift(not x_first, i)(terms[i].astype(jnp.bfloat16)).astype(jnp.float32)
        return result

    cut = TBC * 7 // 13 * BLK
    coefficients = jnp.concatenate(
        [scatter(0, cut, left, True), scatter(cut, cols - cut, turned, False)], axis=1
    )
    return basis, coefficients


def solution(mesh):
    in_specs = (
        P(("rows", "cols"), None, None),
        P(("rows", "cols"), None),
        P(("rows", "cols")),
        P("cols", None),
    )
    out_specs = (P("rows", "cols"), P("rows", "cols"))
    return jax.shard_map(
        on_device, mesh=mesh, in_specs=in_specs, out_specs=out_specs, check_vma=False
    )
```

```python
import functools
import math

import jax
import jax.numpy as jnp
from jax import lax
from jax.experimental import pallas as pl
from jax.experimental.pallas import tpu as pltpu
from jax.sharding import PartitionSpec as P

PBR = 4
TBC = 104
BLK = 128
HIGHEST = lax.Precision.HIGHEST
MIB = 1 << 20


def bucket_kernel(place_ref, blocks_ref, out_ref, sem):
    count = blocks_ref.shape[0]

    def issue(slot, carry):
        pltpu.make_async_copy(blocks_ref.at[slot], out_ref.at[place_ref[slot]], sem).start()
        return carry

    lax.fori_loop(0, count, issue, 0)
    pltpu.make_async_copy(blocks_ref, out_ref.at[pl.ds(0, count)], sem).wait()


def bucket(place, blocks, slots):
    return pl.pallas_call(
        bucket_kernel,
        grid_spec=pltpu.PrefetchScalarGridSpec(
            num_scalar_prefetch=1,
            grid=(),
            in_specs=[pl.BlockSpec(memory_space=pltpu.VMEM)],
            out_specs=pl.BlockSpec(memory_space=pl.ANY),
            scratch_shapes=[pltpu.SemaphoreType.DMA],
        ),
        out_shape=jax.ShapeDtypeStruct((slots,) + blocks.shape[1:], blocks.dtype),
        compiler_params=pltpu.CompilerParams(vmem_limit_bytes=56 * MIB),
        cost_estimate=pl.CostEstimate(flops=0, bytes_accessed=2 * blocks.size * 2, transcendentals=0),
        name="bucket",
    )(place, blocks)


def tile_kernel(code_ref, got_hbm, omega_hbm, tile_hbm, sketch_ref, got, omega, tile, total, sems):
    slots = got.shape[0]
    rows, cols = tile.shape
    get_blocks = pltpu.make_async_copy(got_hbm, got, sems.at[0])
    get_omega = pltpu.make_async_copy(omega_hbm, omega, sems.at[1])
    get_blocks.start()
    get_omega.start()

    def clear(step, carry):
        tile[pl.ds(pl.multiple_of(step * 16, 16), 16), :] = jnp.zeros((16, cols), tile.dtype)
        return carry

    lax.fori_loop(0, rows // 16, clear, 0)
    get_blocks.wait()

    def insert(step, carry):
        code = code_ref[step]
        slot = code & 255
        row = pl.multiple_of(((code >> 8) & 3) * BLK, BLK)
        col = pl.multiple_of(((code >> 10) & 127) * BLK, BLK)
        again = (code >> 17) & 1
        later = (code >> 18) & 1

        @pl.when(again == 0)
        def _():
            tile[pl.ds(row, BLK), pl.ds(col, BLK)] = got[slot]

        @pl.when(again == 1)
        def _():
            @pl.when(later == 0)
            def _():
                total[...] = got[code_ref[step - 1] & 255].astype(jnp.float32)

            value = total[...] + got[slot].astype(jnp.float32)
            total[...] = value
            tile[pl.ds(row, BLK), pl.ds(col, BLK)] = value.astype(tile.dtype)

        return carry

    lax.fori_loop(0, code_ref[slots], insert, 0)
    put_tile = pltpu.make_async_copy(tile, tile_hbm, sems.at[2])
    put_tile.start()
    get_omega.wait()
    sketch_ref[...] = jnp.zeros_like(sketch_ref)
    depth = 1024

    def multiply(step, carry):
        at = pl.ds(pl.multiple_of(step * depth, depth), depth)
        sketch_ref[...] += jnp.dot(tile[:, at], omega[at, :], preferred_element_type=jnp.float32)
        return carry

    lax.fori_loop(0, cols // depth, multiply, 0)
    put_tile.wait()


def tile_and_sketch(code, got, omega, rows, cols):
    slots, rank = got.shape[0], omega.shape[1]
    return pl.pallas_call(
        tile_kernel,
        grid_spec=pltpu.PrefetchScalarGridSpec(
            num_scalar_prefetch=1,
            grid=(),
            in_specs=[pl.BlockSpec(memory_space=pl.ANY)] * 2,
            out_specs=[
                pl.BlockSpec(memory_space=pl.ANY),
                pl.BlockSpec(memory_space=pltpu.VMEM),
            ],
            scratch_shapes=[
                pltpu.VMEM((slots, BLK, BLK), jnp.bfloat16),
                pltpu.VMEM((cols, rank), jnp.bfloat16),
                pltpu.VMEM((rows, cols), jnp.bfloat16),
                pltpu.VMEM((BLK, BLK), jnp.float32),
                pltpu.SemaphoreType.DMA((3,)),
            ],
        ),
        out_shape=[
            jax.ShapeDtypeStruct((rows, cols), jnp.bfloat16),
            jax.ShapeDtypeStruct((rows, rank), jnp.float32),
        ],
        compiler_params=pltpu.CompilerParams(vmem_limit_bytes=52 * MIB),
        cost_estimate=pl.CostEstimate(
            flops=2 * rows * cols * rank,
            bytes_accessed=2 * (got.size + omega.size + rows * cols),
            transcendentals=0,
        ),
        name="tile_and_sketch",
    )(code, got, omega)


def upper_rows(n):
    start = 0
    for at in range(0, n, BLK):
        yield at, start, n - at
        start += n - at


def gram_kernel(core_ref, parts_ref, share_ref, keep_ref, send_ref, packed):
    share = parts_ref[0]
    for i in range(1, parts_ref.shape[0]):
        share += parts_ref[i]
    share_ref[...] = share
    for at, start, width in upper_rows(share.shape[1]):
        packed[:, start : start + width] = lax.dot_general(
            share[:, at : at + BLK],
            share[:, at:],
            (((0,), (0,)), ((), ())),
            precision=HIGHEST,
            preferred_element_type=jnp.float32,
        )
    half = keep_ref.shape[0]
    keep_ref[...] = packed[pl.ds(pl.multiple_of(core_ref[0] * half, half), half), :]
    send_ref[...] = packed[pl.ds(pl.multiple_of((1 - core_ref[0]) * half, half), half), :]


def share_and_gram(core, parts):
    _, share, rank = parts.shape
    packed = sum(width for _, _, width in upper_rows(rank))
    whole = pl.BlockSpec(memory_space=pltpu.VMEM)
    return pl.pallas_call(
        gram_kernel,
        grid_spec=pltpu.PrefetchScalarGridSpec(
            num_scalar_prefetch=1,
            grid=(),
            in_specs=[whole],
            out_specs=[whole] * 3,
            scratch_shapes=[pltpu.VMEM((BLK, packed), jnp.float32)],
        ),
        out_shape=[
            jax.ShapeDtypeStruct((share, rank), jnp.float32),
            jax.ShapeDtypeStruct((BLK // 2, packed), jnp.float32),
            jax.ShapeDtypeStruct((BLK // 2, packed), jnp.float32),
        ],
        compiler_params=pltpu.CompilerParams(vmem_limit_bytes=24 * MIB),
        cost_estimate=pl.CostEstimate(
            flops=12 * share * rank * rank, bytes_accessed=8 * parts.size, transcendentals=0
        ),
        name="share_and_gram",
    )(core, parts)


def factor_kernel(scale, core_ref, mine_ref, other_ref, out_ref, work):
    n = work.shape[0]
    work[...] = jnp.zeros_like(work)
    for at, start, width in upper_rows(n):
        for core, rows_ref in ((core_ref[0], mine_ref), (1 - core_ref[0], other_ref)):
            half = rows_ref.shape[0]
            rows = pl.ds(pl.multiple_of(at + core * half, half), half)
            work[rows, at:] = rows_ref[:, start : start + width] * scale
    row = lax.broadcasted_iota(jnp.int32, (n, n), 0)
    lane = lax.broadcasted_iota(jnp.int32, (n, n), 1)
    out_ref[...] = jnp.where(row == lane, 1.0, 0.0)
    sub = lax.broadcasted_iota(jnp.int32, (8, BLK), 0)
    lane8 = lax.broadcasted_iota(jnp.int32, (8, BLK), 1)
    groups = BLK // 8

    def spread(value, j):
        return jnp.broadcast_to(value[:, j : j + 1], (8, BLK))

    def block(panel, carry):
        at = pl.ds(pl.multiple_of(panel * BLK, BLK), BLK)
        left = [work[pl.ds(pl.multiple_of(panel * BLK + 8 * g, 8), 8), at] for g in range(groups)]
        right = [jnp.where(lane8 == sub + 8 * g, 1.0, 0.0) for g in range(groups)]
        for g0 in range(groups):
            own = [spread(left[g0], 8 * g0 + k) for k in range(8)]
            factors, pivots_left, pivots_right = {}, [], []
            for k in range(8):
                inverse = 1.0 / own[k][k : k + 1, :]
                for later in range(k + 1, 8):
                    factors[k, later] = own[later][k : k + 1, :] * inverse
                    own[later] = own[later] - own[k] * factors[k, later]
                pivots_left.append(left[g0][k : k + 1, :] * inverse)
                pivots_right.append(right[g0][k : k + 1, :] * inverse)
                column = jnp.where(sub > k, own[k], 0.0)
                left[g0] = left[g0] - column * pivots_left[k]
                right[g0] = right[g0] - column * pivots_right[k]
            for g in range(g0 + 1, groups):
                below = [spread(left[g], 8 * g0 + k) for k in range(8)]
                for k in range(8):
                    for later in range(k + 1, 8):
                        below[later] = below[later] - below[k] * factors[k, later]
                    left[g] = left[g] - below[k] * pivots_left[k]
                    right[g] = right[g] - below[k] * pivots_right[k]
        halves = []
        for g in range(groups):
            pivot = jnp.sum(
                jnp.where(lane8 == sub + 8 * g, left[g], 0.0), axis=1, keepdims=True
            )
            halves.append(right[g] * (1.0 / jnp.sqrt(pivot)))
        inverse_block = jnp.concatenate(halves, axis=0)
        both = jnp.concatenate([work[at, :], out_ref[at, :]], axis=1)
        upper = jnp.dot(inverse_block, both, precision=HIGHEST, preferred_element_type=jnp.float32)

        @pl.when(panel < n // BLK - 1)
        def _():
            lanes = lax.broadcasted_iota(jnp.int32, (BLK, n), 1)
            later = jnp.where(lanes >= (panel + 1) * BLK, upper[:, :n], 0.0)
            change = lax.dot_general(
                later, upper, (((0,), (0,)), ((), ())), precision=HIGHEST, preferred_element_type=jnp.float32
            )
            work[...] -= change[:, :n]
            out_ref[...] -= change[:, n:]

        out_ref[at, :] = upper[:, n:]
        return carry

    lax.fori_loop(0, n // BLK, block, 0)


def inverse_factor(core, mine, other, n, scale):
    whole = pl.BlockSpec(memory_space=pltpu.VMEM)
    return pl.pallas_call(
        functools.partial(factor_kernel, scale),
        grid_spec=pltpu.PrefetchScalarGridSpec(
            num_scalar_prefetch=1,
            grid=(),
            in_specs=[whole] * 2,
            out_specs=whole,
            scratch_shapes=[pltpu.VMEM((n, n), jnp.float32)],
        ),
        out_shape=jax.ShapeDtypeStruct((n, n), jnp.float32),
        compiler_params=pltpu.CompilerParams(vmem_limit_bytes=24 * MIB),
        cost_estimate=pl.CostEstimate(
            flops=1 << 35, bytes_accessed=2 * n * n * 4, transcendentals=0
        ),
        name="inverse_factor",
    )(core, mine, other)


FAR = 2
FORWARD = ((2, 0), (2, 1)) + tuple((1, e) for e in range(4))
BACKWARD = ((2, 2), (2, 3)) + tuple((3, e) for e in range(4))
STAY = tuple((0, e) for e in range(4))
PIECES = FORWARD + BACKWARD + STAY


def basis_kernel(at_ref, inverse_ref, own_ref, other_ref, left_ref, turned_ref, basis_ref, chosen):
    pieces = len(PIECES)
    size = chosen.shape[0] // pieces
    panel = own_ref.shape[0]
    for k in range(pieces):
        chosen[k * size : (k + 1) * size, :] = inverse_ref[
            pl.ds(pl.multiple_of(at_ref[k], size), size), :
        ]
    contract = (((1,), (1,)), ((), ()))
    for i, sketch_ref in enumerate((own_ref, other_ref)):
        left = lax.dot_general(
            chosen[...], sketch_ref[...], contract, precision=HIGHEST, preferred_element_type=jnp.float32
        ).astype(left_ref.dtype)
        left_ref[:, i * panel : (i + 1) * panel] = left
        turned_ref[:, i * panel : (i + 1) * panel] = jnp.concatenate(
            [left[PIECES.index((b, a)) * size :][:size] for a, b in PIECES], axis=0
        )
    width = basis_ref.shape[1]
    basis_ref[...] = lax.dot_general(
        own_ref[...],
        inverse_ref[pl.ds(pl.multiple_of(at_ref[pieces], width), width), :],
        contract,
        precision=HIGHEST,
        preferred_element_type=jnp.float32,
    ).astype(basis_ref.dtype)


def basis_parts(at, inverse, own, other, half, width):
    panel, rank = own.shape
    whole = pl.BlockSpec(memory_space=pltpu.VMEM)
    return pl.pallas_call(
        basis_kernel,
        grid_spec=pltpu.PrefetchScalarGridSpec(
            num_scalar_prefetch=1,
            grid=(),
            in_specs=[whole] * 3,
            out_specs=[whole] * 3,
            scratch_shapes=[pltpu.VMEM((half, rank), jnp.float32)],
        ),
        out_shape=[
            jax.ShapeDtypeStruct((half, 2 * panel), jnp.bfloat16),
            jax.ShapeDtypeStruct((half, 2 * panel), jnp.bfloat16),
            jax.ShapeDtypeStruct((panel, width), jnp.bfloat16),
        ],
        compiler_params=pltpu.CompilerParams(vmem_limit_bytes=32 * MIB),
        cost_estimate=pl.CostEstimate(
            flops=12 * rank * panel * (2 * half + width), bytes_accessed=6 * rank * panel, transcendentals=0
        ),
        name="basis_parts",
    )(at, inverse, own, other)


def product_kernel(scale, left_ref, own_ref, other_ref, *out_refs):
    rows = own_ref.shape[0]
    total = jnp.dot(left_ref[:, :rows], own_ref[...], preferred_element_type=jnp.float32)
    total += jnp.dot(left_ref[:, rows:], other_ref[...], preferred_element_type=jnp.float32)
    total *= scale
    start = 0
    for out_ref in out_refs:
        end = start + out_ref.shape[0]
        out_ref[...] = total[start:end].astype(out_ref.dtype)
        start = end


def product(left, own, other, first, width, steps, scale):
    rows = own.shape[0]
    half = left.shape[0]
    count = width * steps
    size = half // len(PIECES)
    heights = [size * len(g) for g in (FORWARD, BACKWARD, STAY)]
    spec = pl.BlockSpec(
        (pl.Element(rows), pl.Element(width)), lambda k: (0, pl.multiple_of(first + k * width, BLK))
    )
    return pl.pallas_call(
        functools.partial(product_kernel, scale),
        grid=(steps,),
        in_specs=[pl.BlockSpec((half, 2 * rows), lambda k: (0, 0)), spec, spec],
        out_specs=[pl.BlockSpec((height, width), lambda k: (0, k)) for height in heights],
        out_shape=[
            jax.ShapeDtypeStruct((height, count), jnp.float32 if i == 2 else jnp.bfloat16)
            for i, height in enumerate(heights)
        ],
        compiler_params=pltpu.CompilerParams(vmem_limit_bytes=40 * MIB),
        cost_estimate=pl.CostEstimate(
            flops=4 * half * rows * count,
            bytes_accessed=(4 * rows + 2 * half) * count,
            transcendentals=0,
        ),
        name="product",
    )(left, own, other)


def on_device(blocks, owner, block_pos, omega):
    slot_count = blocks.shape[0]
    rank = omega.shape[1]
    chips = lax.axis_size("chips")
    row_devices = 2 * chips
    col_devices = lax.axis_size("cols")
    devices_all = row_devices * col_devices
    everywhere = ("chips", "core", "cols")
    capacity = max(2, 2 * slot_count // devices_all)
    slots = devices_all * capacity
    panel, cols = PBR * BLK, TBC * BLK
    total_rows = panel * row_devices
    core = lax.axis_index("core")
    swap = functools.partial(lax.ppermute, axis_name="core", perm=[(0, 1), (1, 0)])

    target = owner[:, 0]
    numbers = jnp.arange(slot_count, dtype=jnp.int32)
    same = (target[:, None] == target[None, :]) & (numbers[None, :] < numbers[:, None])
    place = target * capacity + jnp.sum(same.astype(jnp.int32), axis=1)
    spots = jnp.arange(slots, dtype=jnp.int32)
    hit = place[None, :] == spots[:, None]
    send_where = jnp.sum(jnp.where(hit, block_pos[None, :] + 1, 0), axis=1)
    send_blocks = bucket(place, blocks, slots)
    got_blocks = lax.all_to_all(
        send_blocks.reshape(devices_all, capacity, BLK, BLK), everywhere, 0, 0, tiled=True
    ).reshape(slots, BLK, BLK)
    got_where = lax.all_to_all(
        send_where.reshape(devices_all, capacity), everywhere, 0, 0, tiled=True
    ).reshape(slots)

    key = jnp.where(got_where == 0, PBR * TBC, got_where - 1)
    before = (key[None, :] < key[:, None]) | (
        (key[None, :] == key[:, None]) & (spots[None, :] < spots[:, None])
    )
    order = jnp.sum(before.astype(jnp.int32), axis=1)
    packed = key * slots + spots
    ordered = jnp.sum(jnp.where(order[None, :] == spots[:, None], packed[None, :], 0), axis=1)
    slot, where = ordered % slots, ordered // slots
    again = jnp.concatenate([jnp.zeros((1,), jnp.int32), (where[1:] == where[:-1]).astype(jnp.int32)])
    later = jnp.concatenate([jnp.zeros((1,), jnp.int32), again[:-1]])
    code = slot + (where // TBC) * 256 + (where % TBC) * 1024 + (again << 17) + (later << 18)
    filled = jnp.sum((key < PBR * TBC).astype(jnp.int32))
    code = jnp.concatenate([code, filled[None]])

    tile, part = tile_and_sketch(code, got_blocks, omega, panel, cols)
    other_tile = swap(tile)

    share = panel // col_devices
    parts = lax.all_to_all(part.reshape(col_devices, share, rank), "cols", 0, 0, tiled=True)
    which = core.astype(jnp.int32)[None]
    own_share, keep, send = share_and_gram(which, parts)
    same_core = ("chips", "cols")
    gram_rows = (chips * col_devices, BLK // devices_all, keep.shape[1])
    grams = lax.all_to_all((keep + swap(send)).reshape(gram_rows), same_core, 0, 0, tiled=True)
    gram, late_share = lax.optimization_barrier(
        (jnp.broadcast_to(jnp.sum(grams, axis=0)[None], gram_rows), own_share)
    )
    gram = lax.all_to_all(gram, same_core, 0, 0, tiled=True).reshape(keep.shape)
    other_gram = swap(gram)
    shares = [late_share] + [
        lax.ppermute(late_share, "cols", [(i, (i + d) % col_devices) for i in range(col_devices)])
        for d in range(1, col_devices)
    ]
    back = jnp.stack(shares[::-1] * 2)
    start = col_devices - 1 - lax.axis_index("cols")
    sketch = lax.dynamic_slice_in_dim(back, start, col_devices, 0).reshape(panel, rank)
    other_sketch = swap(sketch)
    inverse = inverse_factor(which, gram, other_gram, rank, 1.0 / total_rows)

    ranks = rank // row_devices
    along = math.isqrt(chips)
    chip = lax.axis_index("chips")
    x, y = chip // along, chip % along
    at = [(((x + a) % along * along + (y + b) % along) * 2 + core) * ranks for a, b in PIECES]
    width = rank // col_devices
    at.append(lax.axis_index("cols") * width)
    left, turned, basis = basis_parts(
        jnp.stack(at).astype(jnp.int32), inverse, sketch, other_sketch, rank // 2, width
    )

    def shift(over_x, steps):
        moves = []
        for i in range(chips):
            a, b = divmod(i, along)
            a, b = ((a + steps) % along, b) if over_x else (a, (b + steps) % along)
            moves.append((i, a * along + b))
        return functools.partial(lax.ppermute, axis_name="chips", perm=moves)

    def multiply(first, count, factor):
        return product(factor, tile, other_tile, first, count // 2, 2, 1.0 / math.sqrt(total_rows))

    def scatter(ahead, behind, total, x_first):
        forward, backward = shift(x_first, 1), shift(x_first, -1)
        ahead, behind = forward(ahead), backward(behind)
        far, back_far = forward(ahead[: FAR * ranks]), backward(behind[: FAR * ranks])
        total += ahead[FAR * ranks :].astype(jnp.float32) + behind[FAR * ranks :].astype(jnp.float32)
        total += jnp.concatenate([far, back_far], axis=0).astype(jnp.float32)
        terms = [total[i * ranks : (i + 1) * ranks] for i in range(along)]
        result = terms[0]
        for i in range(1, along):
            result += shift(not x_first, i)(terms[i].astype(jnp.bfloat16)).astype(jnp.float32)
        return result

    cut = TBC // 2 * BLK
    one = multiply(0, cut, left)
    two = multiply(cut, cols - cut, turned)
    coefficients = jnp.concatenate([scatter(*one, True), scatter(*two, False)], axis=1)
    return basis, coefficients


def solution(mesh):
    rows, cols = mesh.devices.shape
    mesh = jax.sharding.Mesh(mesh.devices.reshape(rows // 2, 2, cols), ("chips", "core", "cols"))
    everywhere = ("chips", "core", "cols")
    in_specs = (P(everywhere, None, None), P(everywhere, None), P(everywhere), P("cols", None))
    out_specs = (P(("chips", "core"), "cols"), P(("chips", "core"), "cols"))
    return jax.shard_map(
        on_device, mesh=mesh, in_specs=in_specs, out_specs=out_specs, check_vma=False
    )
```

```python
import functools
import math

import jax
import jax.numpy as jnp
import numpy as np
from jax import lax
from jax.experimental import pallas as pl
from jax.experimental.pallas import tpu as pltpu
from jax.sharding import PartitionSpec as P

PBR = 4
TBC = 104
BLK = 128
HIGHEST = lax.Precision.HIGHEST
MIB = 1 << 20


def bucket_kernel(place_ref, blocks_ref, out_ref, sem):
    count = blocks_ref.shape[0]

    def issue(slot, carry):
        pltpu.make_async_copy(blocks_ref.at[slot], out_ref.at[place_ref[slot]], sem).start()
        return carry

    lax.fori_loop(0, count, issue, 0)
    pltpu.make_async_copy(blocks_ref, out_ref.at[pl.ds(0, count)], sem).wait()


def bucket(place, blocks, slots):
    return pl.pallas_call(
        bucket_kernel,
        grid_spec=pltpu.PrefetchScalarGridSpec(
            num_scalar_prefetch=1,
            grid=(),
            in_specs=[pl.BlockSpec(memory_space=pltpu.VMEM)],
            out_specs=pl.BlockSpec(memory_space=pl.ANY),
            scratch_shapes=[pltpu.SemaphoreType.DMA],
        ),
        out_shape=jax.ShapeDtypeStruct((slots,) + blocks.shape[1:], blocks.dtype),
        compiler_params=pltpu.CompilerParams(vmem_limit_bytes=56 * MIB),
        cost_estimate=pl.CostEstimate(flops=0, bytes_accessed=2 * blocks.size * 2, transcendentals=0),
        name="bucket",
    )(place, blocks)


def tile_kernel(code_ref, got_hbm, omega_hbm, tile_hbm, sketch_ref, got, omega, tile, total, sems):
    slots = got.shape[0]
    rows, cols = tile.shape
    get_blocks = pltpu.make_async_copy(got_hbm, got, sems.at[0])
    get_omega = pltpu.make_async_copy(omega_hbm, omega, sems.at[1])
    get_blocks.start()
    get_omega.start()

    def clear(step, carry):
        tile[pl.ds(pl.multiple_of(step * 16, 16), 16), :] = jnp.zeros((16, cols), tile.dtype)
        return carry

    lax.fori_loop(0, rows // 16, clear, 0)
    get_blocks.wait()

    def insert(step, carry):
        code = code_ref[step]
        slot = code & 255
        row = pl.multiple_of(((code >> 8) & 3) * BLK, BLK)
        col = pl.multiple_of(((code >> 10) & 127) * BLK, BLK)
        again = (code >> 17) & 1
        later = (code >> 18) & 1

        @pl.when(again == 0)
        def _():
            tile[pl.ds(row, BLK), pl.ds(col, BLK)] = got[slot]

        @pl.when(again == 1)
        def _():
            @pl.when(later == 0)
            def _():
                total[...] = got[code_ref[step - 1] & 255].astype(jnp.float32)

            value = total[...] + got[slot].astype(jnp.float32)
            total[...] = value
            tile[pl.ds(row, BLK), pl.ds(col, BLK)] = value.astype(tile.dtype)

        return carry

    lax.fori_loop(0, code_ref[slots], insert, 0)
    put_tile = pltpu.make_async_copy(tile, tile_hbm, sems.at[2])
    put_tile.start()
    get_omega.wait()
    sketch_ref[...] = jnp.zeros_like(sketch_ref)
    depth = 1024

    def multiply(step, carry):
        at = pl.ds(pl.multiple_of(step * depth, depth), depth)
        sketch_ref[...] += jnp.dot(tile[:, at], omega[at, :], preferred_element_type=jnp.float32)
        return carry

    lax.fori_loop(0, cols // depth, multiply, 0)
    put_tile.wait()


def tile_and_sketch(code, got, omega, rows, cols):
    slots, rank = got.shape[0], omega.shape[1]
    return pl.pallas_call(
        tile_kernel,
        grid_spec=pltpu.PrefetchScalarGridSpec(
            num_scalar_prefetch=1,
            grid=(),
            in_specs=[pl.BlockSpec(memory_space=pl.ANY)] * 2,
            out_specs=[
                pl.BlockSpec(memory_space=pl.ANY),
                pl.BlockSpec(memory_space=pltpu.VMEM),
            ],
            scratch_shapes=[
                pltpu.VMEM((slots, BLK, BLK), jnp.bfloat16),
                pltpu.VMEM((cols, rank), jnp.bfloat16),
                pltpu.VMEM((rows, cols), jnp.bfloat16),
                pltpu.VMEM((BLK, BLK), jnp.float32),
                pltpu.SemaphoreType.DMA((3,)),
            ],
        ),
        out_shape=[
            jax.ShapeDtypeStruct((rows, cols), jnp.bfloat16),
            jax.ShapeDtypeStruct((rows, rank), jnp.float32),
        ],
        compiler_params=pltpu.CompilerParams(vmem_limit_bytes=52 * MIB),
        cost_estimate=pl.CostEstimate(
            flops=2 * rows * cols * rank,
            bytes_accessed=2 * (got.size + omega.size + rows * cols),
            transcendentals=0,
        ),
        name="tile_and_sketch",
    )(code, got, omega)


def upper_rows(n):
    start = 0
    for at in range(0, n, BLK):
        yield at, start, n - at
        start += n - at


def gram_kernel(core_ref, parts_ref, share_ref, keep_ref, send_ref, packed):
    share = parts_ref[0]
    for i in range(1, parts_ref.shape[0]):
        share += parts_ref[i]
    share_ref[...] = share
    for at, start, width in upper_rows(share.shape[1]):
        packed[:, start : start + width] = lax.dot_general(
            share[:, at : at + BLK],
            share[:, at:],
            (((0,), (0,)), ((), ())),
            precision=HIGHEST,
            preferred_element_type=jnp.float32,
        )
    half = keep_ref.shape[0]
    keep_ref[...] = packed[pl.ds(pl.multiple_of(core_ref[0] * half, half), half), :]
    send_ref[...] = packed[pl.ds(pl.multiple_of((1 - core_ref[0]) * half, half), half), :]


def share_and_gram(core, parts):
    _, share, rank = parts.shape
    packed = sum(width for _, _, width in upper_rows(rank))
    whole = pl.BlockSpec(memory_space=pltpu.VMEM)
    return pl.pallas_call(
        gram_kernel,
        grid_spec=pltpu.PrefetchScalarGridSpec(
            num_scalar_prefetch=1,
            grid=(),
            in_specs=[whole],
            out_specs=[whole] * 3,
            scratch_shapes=[pltpu.VMEM((BLK, packed), jnp.float32)],
        ),
        out_shape=[
            jax.ShapeDtypeStruct((share, rank), jnp.float32),
            jax.ShapeDtypeStruct((BLK // 2, packed), jnp.float32),
            jax.ShapeDtypeStruct((BLK // 2, packed), jnp.float32),
        ],
        compiler_params=pltpu.CompilerParams(vmem_limit_bytes=24 * MIB),
        cost_estimate=pl.CostEstimate(
            flops=12 * share * rank * rank, bytes_accessed=8 * parts.size, transcendentals=0
        ),
        name="share_and_gram",
    )(core, parts)


def factor_kernel(scale, core_ref, mine_ref, other_ref, out_ref, work):
    n = work.shape[0]
    work[...] = jnp.zeros_like(work)
    for at, start, width in upper_rows(n):
        for core, rows_ref in ((core_ref[0], mine_ref), (1 - core_ref[0], other_ref)):
            half = rows_ref.shape[0]
            rows = pl.ds(pl.multiple_of(at + core * half, half), half)
            work[rows, at:] = rows_ref[:, start : start + width] * scale
    row = lax.broadcasted_iota(jnp.int32, (n, n), 0)
    lane = lax.broadcasted_iota(jnp.int32, (n, n), 1)
    out_ref[...] = jnp.where(row == lane, 1.0, 0.0)
    sub = lax.broadcasted_iota(jnp.int32, (8, BLK), 0)
    lane8 = lax.broadcasted_iota(jnp.int32, (8, BLK), 1)
    groups = BLK // 8

    def spread(value, j):
        return jnp.broadcast_to(value[:, j : j + 1], (8, BLK))

    def block(panel, carry):
        at = pl.ds(pl.multiple_of(panel * BLK, BLK), BLK)
        left = [work[pl.ds(pl.multiple_of(panel * BLK + 8 * g, 8), 8), at] for g in range(groups)]
        right = [jnp.where(lane8 == sub + 8 * g, 1.0, 0.0) for g in range(groups)]
        for g0 in range(groups):
            own = [spread(left[g0], 8 * g0 + k) for k in range(8)]
            factors, pivots_left, pivots_right = {}, [], []
            for k in range(8):
                inverse = 1.0 / own[k][k : k + 1, :]
                for later in range(k + 1, 8):
                    factors[k, later] = own[later][k : k + 1, :] * inverse
                    own[later] = own[later] - own[k] * factors[k, later]
                pivots_left.append(left[g0][k : k + 1, :] * inverse)
                pivots_right.append(right[g0][k : k + 1, :] * inverse)
                column = jnp.where(sub > k, own[k], 0.0)
                left[g0] = left[g0] - column * pivots_left[k]
                right[g0] = right[g0] - column * pivots_right[k]
            for g in range(g0 + 1, groups):
                below = [spread(left[g], 8 * g0 + k) for k in range(8)]
                for k in range(8):
                    for later in range(k + 1, 8):
                        below[later] = below[later] - below[k] * factors[k, later]
                    left[g] = left[g] - below[k] * pivots_left[k]
                    right[g] = right[g] - below[k] * pivots_right[k]
        halves = []
        for g in range(groups):
            pivot = jnp.sum(
                jnp.where(lane8 == sub + 8 * g, left[g], 0.0), axis=1, keepdims=True
            )
            halves.append(right[g] * (1.0 / jnp.sqrt(pivot)))
        inverse_block = jnp.concatenate(halves, axis=0)
        both = jnp.concatenate([work[at, :], out_ref[at, :]], axis=1)
        upper = jnp.dot(inverse_block, both, precision=HIGHEST, preferred_element_type=jnp.float32)

        @pl.when(panel < n // BLK - 1)
        def _():
            lanes = lax.broadcasted_iota(jnp.int32, (BLK, n), 1)
            later = jnp.where(lanes >= (panel + 1) * BLK, upper[:, :n], 0.0)
            change = lax.dot_general(
                later, upper, (((0,), (0,)), ((), ())), precision=HIGHEST, preferred_element_type=jnp.float32
            )
            work[...] -= change[:, :n]
            out_ref[...] -= change[:, n:]

        out_ref[at, :] = upper[:, n:]
        return carry

    lax.fori_loop(0, n // BLK, block, 0)


def inverse_factor(core, mine, other, n, scale):
    whole = pl.BlockSpec(memory_space=pltpu.VMEM)
    return pl.pallas_call(
        functools.partial(factor_kernel, scale),
        grid_spec=pltpu.PrefetchScalarGridSpec(
            num_scalar_prefetch=1,
            grid=(),
            in_specs=[whole] * 2,
            out_specs=whole,
            scratch_shapes=[pltpu.VMEM((n, n), jnp.float32)],
        ),
        out_shape=jax.ShapeDtypeStruct((n, n), jnp.float32),
        compiler_params=pltpu.CompilerParams(vmem_limit_bytes=24 * MIB),
        cost_estimate=pl.CostEstimate(
            flops=1 << 35, bytes_accessed=2 * n * n * 4, transcendentals=0
        ),
        name="inverse_factor",
    )(core, mine, other)


FAR = 2
FORWARD = ((2, 0), (2, 1)) + tuple((1, e) for e in range(4))
BACKWARD = ((2, 2), (2, 3)) + tuple((3, e) for e in range(4))
STAY = tuple((0, e) for e in range(4))
PIECES = FORWARD + BACKWARD + STAY


def basis_kernel(at_ref, inverse_ref, own_ref, other_ref, left_ref, turned_ref, basis_ref, chosen):
    pieces = len(PIECES)
    size = chosen.shape[0] // pieces
    panel = own_ref.shape[0]
    for k in range(pieces):
        chosen[k * size : (k + 1) * size, :] = inverse_ref[
            pl.ds(pl.multiple_of(at_ref[k], size), size), :
        ]
    contract = (((1,), (1,)), ((), ()))
    for i, sketch_ref in enumerate((own_ref, other_ref)):
        left = lax.dot_general(
            chosen[...], sketch_ref[...], contract, precision=HIGHEST, preferred_element_type=jnp.float32
        ).astype(left_ref.dtype)
        left_ref[:, i * panel : (i + 1) * panel] = left
        turned_ref[:, i * panel : (i + 1) * panel] = jnp.concatenate(
            [left[PIECES.index((b, a)) * size :][:size] for a, b in PIECES], axis=0
        )
    width = basis_ref.shape[1]
    basis_ref[...] = lax.dot_general(
        own_ref[...],
        inverse_ref[pl.ds(pl.multiple_of(at_ref[pieces], width), width), :],
        contract,
        precision=HIGHEST,
        preferred_element_type=jnp.float32,
    ).astype(basis_ref.dtype)


def basis_parts(at, inverse, own, other, half, width):
    panel, rank = own.shape
    whole = pl.BlockSpec(memory_space=pltpu.VMEM)
    return pl.pallas_call(
        basis_kernel,
        grid_spec=pltpu.PrefetchScalarGridSpec(
            num_scalar_prefetch=1,
            grid=(),
            in_specs=[whole] * 3,
            out_specs=[whole] * 3,
            scratch_shapes=[pltpu.VMEM((half, rank), jnp.float32)],
        ),
        out_shape=[
            jax.ShapeDtypeStruct((half, 2 * panel), jnp.bfloat16),
            jax.ShapeDtypeStruct((half, 2 * panel), jnp.bfloat16),
            jax.ShapeDtypeStruct((panel, width), jnp.bfloat16),
        ],
        compiler_params=pltpu.CompilerParams(vmem_limit_bytes=32 * MIB),
        cost_estimate=pl.CostEstimate(
            flops=12 * rank * panel * (2 * half + width), bytes_accessed=6 * rank * panel, transcendentals=0
        ),
        name="basis_parts",
    )(at, inverse, own, other)


def product_kernel(scale, left_ref, own_ref, other_ref, *out_refs):
    rows = own_ref.shape[0]
    total = jnp.dot(left_ref[:, :rows], own_ref[...], preferred_element_type=jnp.float32)
    total += jnp.dot(left_ref[:, rows:], other_ref[...], preferred_element_type=jnp.float32)
    total *= scale
    start = 0
    for out_ref in out_refs:
        end = start + out_ref.shape[0]
        out_ref[...] = total[start:end].astype(out_ref.dtype)
        start = end


def product(left, own, other, first, width, steps, scale):
    rows = own.shape[0]
    half = left.shape[0]
    count = width * steps
    size = half // len(PIECES)
    heights = [size * len(g) for g in (FORWARD, BACKWARD, STAY)]
    spec = pl.BlockSpec(
        (pl.Element(rows), pl.Element(width)), lambda k: (0, pl.multiple_of(first + k * width, BLK))
    )
    return pl.pallas_call(
        functools.partial(product_kernel, scale),
        grid=(steps,),
        in_specs=[pl.BlockSpec((half, 2 * rows), lambda k: (0, 0)), spec, spec],
        out_specs=[pl.BlockSpec((height, width), lambda k: (0, k)) for height in heights],
        out_shape=[
            jax.ShapeDtypeStruct((height, count), jnp.float32 if i == 2 else jnp.bfloat16)
            for i, height in enumerate(heights)
        ],
        compiler_params=pltpu.CompilerParams(vmem_limit_bytes=40 * MIB),
        cost_estimate=pl.CostEstimate(
            flops=4 * half * rows * count,
            bytes_accessed=(4 * rows + 2 * half) * count,
            transcendentals=0,
        ),
        name="product",
    )(left, own, other)


def on_device(blocks, owner, block_pos, omega):
    slot_count = blocks.shape[0]
    rank = omega.shape[1]
    chips = lax.axis_size("chips")
    row_devices = 2 * chips
    col_devices = lax.axis_size("cols")
    devices_all = row_devices * col_devices
    everywhere, same_core = ("chips", "core", "cols"), ("chips", "cols")
    capacity = max(2, 2 * slot_count // devices_all)
    slots = devices_all * capacity
    panel, cols = PBR * BLK, TBC * BLK
    total_rows = panel * row_devices
    core = lax.axis_index("core")
    swap = functools.partial(lax.ppermute, axis_name="core", perm=[(0, 1), (1, 0)])

    target = owner[:, 0]
    numbers = jnp.arange(slot_count, dtype=jnp.int32)
    same = (target[:, None] == target[None, :]) & (numbers[None, :] < numbers[:, None])
    place = target * capacity + jnp.sum(same.astype(jnp.int32), axis=1)
    spots = jnp.arange(slots, dtype=jnp.int32)
    by_core = np.arange(slots, dtype=np.int32).reshape(chips, 2, col_devices, capacity)
    by_core = jnp.asarray(by_core.transpose(0, 2, 1, 3).reshape(slots))
    hit = place[None, :] == by_core[:, None]
    send_where = jnp.sum(jnp.where(hit, block_pos[None, :] + 1, 0), axis=1)
    send_blocks = bucket(place, blocks, slots)
    got_blocks = lax.all_to_all(
        send_blocks.reshape(devices_all, capacity, BLK, BLK), everywhere, 0, 0, tiled=True
    ).reshape(slots, BLK, BLK)
    got_where = lax.all_to_all(
        send_where.reshape(devices_all // 2, 2 * capacity), same_core, 0, 0, tiled=True
    ).reshape(devices_all // 2, 2, capacity)
    first, second = got_where[:, 0], got_where[:, 1]
    kept = jnp.where(core == 0, first, second)
    come = swap(jnp.where(core == 0, second, first))
    got_where = jnp.stack(
        [
            jnp.where(core == 0, part, other).reshape(chips, col_devices, capacity)
            for part, other in ((kept, come), (come, kept))
        ],
        axis=1,
    ).reshape(slots)

    key = jnp.where(got_where == 0, PBR * TBC, got_where - 1)
    before = (key[None, :] < key[:, None]) | (
        (key[None, :] == key[:, None]) & (spots[None, :] < spots[:, None])
    )
    order = jnp.sum(before.astype(jnp.int32), axis=1)
    packed = key * slots + spots
    ordered = jnp.sum(jnp.where(order[None, :] == spots[:, None], packed[None, :], 0), axis=1)
    slot, where = ordered % slots, ordered // slots
    again = jnp.concatenate([jnp.zeros((1,), jnp.int32), (where[1:] == where[:-1]).astype(jnp.int32)])
    later = jnp.concatenate([jnp.zeros((1,), jnp.int32), again[:-1]])
    code = slot + (where // TBC) * 256 + (where % TBC) * 1024 + (again << 17) + (later << 18)
    filled = jnp.sum((key < PBR * TBC).astype(jnp.int32))
    code = jnp.concatenate([code, filled[None]])

    tile, part = tile_and_sketch(code, got_blocks, omega, panel, cols)
    other_tile = swap(tile)

    share = panel // col_devices
    parts = lax.all_to_all(part.reshape(col_devices, share, rank), "cols", 0, 0, tiled=True)
    which = core.astype(jnp.int32)[None]
    own_share, keep, send = share_and_gram(which, parts)
    gram_rows = (chips * col_devices, BLK // devices_all, keep.shape[1])
    grams = lax.all_to_all((keep + swap(send)).reshape(gram_rows), same_core, 0, 0, tiled=True)
    gram, late_share = lax.optimization_barrier(
        (jnp.broadcast_to(jnp.sum(grams, axis=0)[None], gram_rows), own_share)
    )
    gram = lax.all_to_all(gram, same_core, 0, 0, tiled=True).reshape(keep.shape)
    other_gram = swap(gram)
    shares = [late_share] + [
        lax.ppermute(late_share, "cols", [(i, (i + d) % col_devices) for i in range(col_devices)])
        for d in range(1, col_devices)
    ]
    back = jnp.stack(shares[::-1] * 2)
    start = col_devices - 1 - lax.axis_index("cols")
    sketch = lax.dynamic_slice_in_dim(back, start, col_devices, 0).reshape(panel, rank)
    other_sketch = swap(sketch)
    inverse = inverse_factor(which, gram, other_gram, rank, 1.0 / total_rows)

    ranks = rank // row_devices
    along = math.isqrt(chips)
    chip = lax.axis_index("chips")
    x, y = chip // along, chip % along
    at = [(((x + a) % along * along + (y + b) % along) * 2 + core) * ranks for a, b in PIECES]
    width = rank // col_devices
    at.append(lax.axis_index("cols") * width)
    left, turned, basis = basis_parts(
        jnp.stack(at).astype(jnp.int32), inverse, sketch, other_sketch, rank // 2, width
    )

    def shift(over_x, steps):
        moves = []
        for i in range(chips):
            a, b = divmod(i, along)
            a, b = ((a + steps) % along, b) if over_x else (a, (b + steps) % along)
            moves.append((i, a * along + b))
        return functools.partial(lax.ppermute, axis_name="chips", perm=moves)

    def multiply(first, count, factor):
        return product(factor, tile, other_tile, first, count // 2, 2, 1.0 / math.sqrt(total_rows))

    def scatter(ahead, behind, total, x_first):
        forward, backward = shift(x_first, 1), shift(x_first, -1)
        ahead, behind = forward(ahead), backward(behind)
        far, back_far = forward(ahead[: FAR * ranks]), backward(behind[: FAR * ranks])
        total += ahead[FAR * ranks :].astype(jnp.float32) + behind[FAR * ranks :].astype(jnp.float32)
        total += jnp.concatenate([far, back_far], axis=0).astype(jnp.float32)
        terms = [total[i * ranks : (i + 1) * ranks] for i in range(along)]
        result = terms[0]
        for i in range(1, along):
            result += shift(not x_first, i)(terms[i].astype(jnp.bfloat16)).astype(jnp.float32)
        return result

    cut = TBC // 2 * BLK
    one = multiply(0, cut, left)
    two = multiply(cut, cols - cut, turned)
    coefficients = jnp.concatenate([scatter(*one, True), scatter(*two, False)], axis=1)
    return basis, coefficients


def solution(mesh):
    rows, cols = mesh.devices.shape
    mesh = jax.sharding.Mesh(mesh.devices.reshape(rows // 2, 2, cols), ("chips", "core", "cols"))
    everywhere = ("chips", "core", "cols")
    in_specs = (P(everywhere, None, None), P(everywhere, None), P(everywhere), P("cols", None))
    out_specs = (P(("chips", "core"), "cols"), P(("chips", "core"), "cols"))
    return jax.shard_map(
        on_device, mesh=mesh, in_specs=in_specs, out_specs=out_specs, check_vma=False
    )
```

```python
import functools
import math

import jax
import jax.numpy as jnp
from jax import lax
from jax.experimental import pallas as pl
from jax.experimental.pallas import tpu as pltpu
from jax.sharding import PartitionSpec as P

PBR = 4
TBC = 104
BLK = 128
HIGHEST = lax.Precision.HIGHEST
MIB = 1 << 20


def bucket_kernel(place_ref, blocks_ref, out_ref, sem):
    count = blocks_ref.shape[0]

    def issue(slot, carry):
        pltpu.make_async_copy(blocks_ref.at[slot], out_ref.at[place_ref[slot]], sem).start()
        return carry

    lax.fori_loop(0, count, issue, 0)
    pltpu.make_async_copy(blocks_ref, out_ref.at[pl.ds(0, count)], sem).wait()


def bucket(place, blocks, slots):
    return pl.pallas_call(
        bucket_kernel,
        grid_spec=pltpu.PrefetchScalarGridSpec(
            num_scalar_prefetch=1,
            grid=(),
            in_specs=[pl.BlockSpec(memory_space=pltpu.VMEM)],
            out_specs=pl.BlockSpec(memory_space=pl.ANY),
            scratch_shapes=[pltpu.SemaphoreType.DMA],
        ),
        out_shape=jax.ShapeDtypeStruct((slots,) + blocks.shape[1:], blocks.dtype),
        compiler_params=pltpu.CompilerParams(vmem_limit_bytes=56 * MIB),
        cost_estimate=pl.CostEstimate(flops=0, bytes_accessed=2 * blocks.size * 2, transcendentals=0),
        name="bucket",
    )(place, blocks)


def tile_kernel(code_ref, got_hbm, omega_hbm, tile_hbm, sketch_ref, got, omega, tile, total, sems):
    slots = got.shape[0]
    rows, cols = tile.shape
    get_blocks = pltpu.make_async_copy(got_hbm, got, sems.at[0])
    get_omega = pltpu.make_async_copy(omega_hbm, omega, sems.at[1])
    get_blocks.start()
    get_omega.start()

    def clear(step, carry):
        tile[pl.ds(pl.multiple_of(step * 16, 16), 16), :] = jnp.zeros((16, cols), tile.dtype)
        return carry

    lax.fori_loop(0, rows // 16, clear, 0)
    get_blocks.wait()

    def insert(step, carry):
        code = code_ref[step]
        slot = code & 255
        row = pl.multiple_of(((code >> 8) & 3) * BLK, BLK)
        col = pl.multiple_of(((code >> 10) & 127) * BLK, BLK)
        again = (code >> 17) & 1
        later = (code >> 18) & 1

        @pl.when(again == 0)
        def _():
            tile[pl.ds(row, BLK), pl.ds(col, BLK)] = got[slot]

        @pl.when(again == 1)
        def _():
            @pl.when(later == 0)
            def _():
                total[...] = got[code_ref[step - 1] & 255].astype(jnp.float32)

            value = total[...] + got[slot].astype(jnp.float32)
            total[...] = value
            tile[pl.ds(row, BLK), pl.ds(col, BLK)] = value.astype(tile.dtype)

        return carry

    lax.fori_loop(0, code_ref[slots], insert, 0)
    put_tile = pltpu.make_async_copy(tile, tile_hbm, sems.at[2])
    put_tile.start()
    get_omega.wait()
    sketch_ref[...] = jnp.zeros_like(sketch_ref)
    depth = 1024

    def multiply(step, carry):
        at = pl.ds(pl.multiple_of(step * depth, depth), depth)
        sketch_ref[...] += jnp.dot(tile[:, at], omega[at, :], preferred_element_type=jnp.float32)
        return carry

    lax.fori_loop(0, cols // depth, multiply, 0)
    put_tile.wait()


def tile_and_sketch(code, got, omega, rows, cols):
    slots, rank = got.shape[0], omega.shape[1]
    return pl.pallas_call(
        tile_kernel,
        grid_spec=pltpu.PrefetchScalarGridSpec(
            num_scalar_prefetch=1,
            grid=(),
            in_specs=[pl.BlockSpec(memory_space=pl.ANY)] * 2,
            out_specs=[
                pl.BlockSpec(memory_space=pl.ANY),
                pl.BlockSpec(memory_space=pltpu.VMEM),
            ],
            scratch_shapes=[
                pltpu.VMEM((slots, BLK, BLK), jnp.bfloat16),
                pltpu.VMEM((cols, rank), jnp.bfloat16),
                pltpu.VMEM((rows, cols), jnp.bfloat16),
                pltpu.VMEM((BLK, BLK), jnp.float32),
                pltpu.SemaphoreType.DMA((3,)),
            ],
        ),
        out_shape=[
            jax.ShapeDtypeStruct((rows, cols), jnp.bfloat16),
            jax.ShapeDtypeStruct((rows, rank), jnp.float32),
        ],
        compiler_params=pltpu.CompilerParams(vmem_limit_bytes=52 * MIB),
        cost_estimate=pl.CostEstimate(
            flops=2 * rows * cols * rank,
            bytes_accessed=2 * (got.size + omega.size + rows * cols),
            transcendentals=0,
        ),
        name="tile_and_sketch",
    )(code, got, omega)


def upper_rows(n):
    start = 0
    for at in range(0, n, BLK):
        yield at, start, n - at
        start += n - at


def gram_kernel(core_ref, parts_ref, share_ref, keep_ref, send_ref, packed):
    share = parts_ref[0]
    for i in range(1, parts_ref.shape[0]):
        share += parts_ref[i]
    share_ref[...] = share
    for at, start, width in upper_rows(share.shape[1]):
        packed[:, start : start + width] = lax.dot_general(
            share[:, at : at + BLK],
            share[:, at:],
            (((0,), (0,)), ((), ())),
            precision=HIGHEST,
            preferred_element_type=jnp.float32,
        )
    half = keep_ref.shape[0]
    keep_ref[...] = packed[pl.ds(pl.multiple_of(core_ref[0] * half, half), half), :]
    send_ref[...] = packed[pl.ds(pl.multiple_of((1 - core_ref[0]) * half, half), half), :]


def share_and_gram(core, parts):
    _, share, rank = parts.shape
    packed = sum(width for _, _, width in upper_rows(rank))
    whole = pl.BlockSpec(memory_space=pltpu.VMEM)
    return pl.pallas_call(
        gram_kernel,
        grid_spec=pltpu.PrefetchScalarGridSpec(
            num_scalar_prefetch=1,
            grid=(),
            in_specs=[whole],
            out_specs=[whole] * 3,
            scratch_shapes=[pltpu.VMEM((BLK, packed), jnp.float32)],
        ),
        out_shape=[
            jax.ShapeDtypeStruct((share, rank), jnp.float32),
            jax.ShapeDtypeStruct((BLK // 2, packed), jnp.float32),
            jax.ShapeDtypeStruct((BLK // 2, packed), jnp.float32),
        ],
        compiler_params=pltpu.CompilerParams(vmem_limit_bytes=24 * MIB),
        cost_estimate=pl.CostEstimate(
            flops=12 * share * rank * rank, bytes_accessed=8 * parts.size, transcendentals=0
        ),
        name="share_and_gram",
    )(core, parts)


def factor_kernel(scale, core_ref, mine_ref, other_ref, out_ref, work):
    n = work.shape[0]
    work[...] = jnp.zeros_like(work)
    for at, start, width in upper_rows(n):
        for core, rows_ref in ((core_ref[0], mine_ref), (1 - core_ref[0], other_ref)):
            half = rows_ref.shape[0]
            rows = pl.ds(pl.multiple_of(at + core * half, half), half)
            work[rows, at:] = rows_ref[:, start : start + width] * scale
    row = lax.broadcasted_iota(jnp.int32, (n, n), 0)
    lane = lax.broadcasted_iota(jnp.int32, (n, n), 1)
    out_ref[...] = jnp.where(row == lane, 1.0, 0.0)
    sub = lax.broadcasted_iota(jnp.int32, (8, BLK), 0)
    lane8 = lax.broadcasted_iota(jnp.int32, (8, BLK), 1)
    groups = BLK // 8

    def spread(value, j):
        return jnp.broadcast_to(value[:, j : j + 1], (8, BLK))

    def block(panel, carry):
        at = pl.ds(pl.multiple_of(panel * BLK, BLK), BLK)
        left = [work[pl.ds(pl.multiple_of(panel * BLK + 8 * g, 8), 8), at] for g in range(groups)]
        right = [jnp.where(lane8 == sub + 8 * g, 1.0, 0.0) for g in range(groups)]
        for g0 in range(groups):
            own = [spread(left[g0], 8 * g0 + k) for k in range(8)]
            factors, pivots_left, pivots_right = {}, [], []
            for k in range(8):
                inverse = 1.0 / own[k][k : k + 1, :]
                for later in range(k + 1, 8):
                    factors[k, later] = own[later][k : k + 1, :] * inverse
                    own[later] = own[later] - own[k] * factors[k, later]
                pivots_left.append(left[g0][k : k + 1, :] * inverse)
                pivots_right.append(right[g0][k : k + 1, :] * inverse)
                column = jnp.where(sub > k, own[k], 0.0)
                left[g0] = left[g0] - column * pivots_left[k]
                right[g0] = right[g0] - column * pivots_right[k]
            for g in range(g0 + 1, groups):
                below = [spread(left[g], 8 * g0 + k) for k in range(8)]
                for k in range(8):
                    for later in range(k + 1, 8):
                        below[later] = below[later] - below[k] * factors[k, later]
                    left[g] = left[g] - below[k] * pivots_left[k]
                    right[g] = right[g] - below[k] * pivots_right[k]
        halves = []
        for g in range(groups):
            pivot = jnp.sum(
                jnp.where(lane8 == sub + 8 * g, left[g], 0.0), axis=1, keepdims=True
            )
            halves.append(right[g] * (1.0 / jnp.sqrt(pivot)))
        inverse_block = jnp.concatenate(halves, axis=0)
        both = jnp.concatenate([work[at, :], out_ref[at, :]], axis=1)
        upper = jnp.dot(inverse_block, both, precision=HIGHEST, preferred_element_type=jnp.float32)

        @pl.when(panel < n // BLK - 1)
        def _():
            lanes = lax.broadcasted_iota(jnp.int32, (BLK, n), 1)
            later = jnp.where(lanes >= (panel + 1) * BLK, upper[:, :n], 0.0)
            change = lax.dot_general(
                later, upper, (((0,), (0,)), ((), ())), precision=HIGHEST, preferred_element_type=jnp.float32
            )
            work[...] -= change[:, :n]
            out_ref[...] -= change[:, n:]

        out_ref[at, :] = upper[:, n:]
        return carry

    lax.fori_loop(0, n // BLK, block, 0)


def inverse_factor(core, mine, other, n, scale):
    whole = pl.BlockSpec(memory_space=pltpu.VMEM)
    return pl.pallas_call(
        functools.partial(factor_kernel, scale),
        grid_spec=pltpu.PrefetchScalarGridSpec(
            num_scalar_prefetch=1,
            grid=(),
            in_specs=[whole] * 2,
            out_specs=whole,
            scratch_shapes=[pltpu.VMEM((n, n), jnp.float32)],
        ),
        out_shape=jax.ShapeDtypeStruct((n, n), jnp.float32),
        compiler_params=pltpu.CompilerParams(vmem_limit_bytes=24 * MIB),
        cost_estimate=pl.CostEstimate(
            flops=1 << 35, bytes_accessed=2 * n * n * 4, transcendentals=0
        ),
        name="inverse_factor",
    )(core, mine, other)


FAR = 2
FORWARD = ((2, 0), (2, 1)) + tuple((1, e) for e in range(4))
BACKWARD = ((2, 2), (2, 3)) + tuple((3, e) for e in range(4))
STAY = tuple((0, e) for e in range(4))
PIECES = FORWARD + BACKWARD + STAY


def basis_kernel(at_ref, inverse_ref, own_ref, other_ref, left_ref, turned_ref, basis_ref, chosen):
    pieces = len(PIECES)
    size = chosen.shape[0] // pieces
    panel = own_ref.shape[0]
    for k in range(pieces):
        chosen[k * size : (k + 1) * size, :] = inverse_ref[
            pl.ds(pl.multiple_of(at_ref[k], size), size), :
        ]
    contract = (((1,), (1,)), ((), ()))
    for i, sketch_ref in enumerate((own_ref, other_ref)):
        left = lax.dot_general(
            chosen[...], sketch_ref[...], contract, precision=HIGHEST, preferred_element_type=jnp.float32
        ).astype(left_ref.dtype)
        left_ref[:, i * panel : (i + 1) * panel] = left
        turned_ref[:, i * panel : (i + 1) * panel] = jnp.concatenate(
            [left[PIECES.index((b, a)) * size :][:size] for a, b in PIECES], axis=0
        )
    width = basis_ref.shape[1]
    basis_ref[...] = lax.dot_general(
        own_ref[...],
        inverse_ref[pl.ds(pl.multiple_of(at_ref[pieces], width), width), :],
        contract,
        precision=HIGHEST,
        preferred_element_type=jnp.float32,
    ).astype(basis_ref.dtype)


def basis_parts(at, inverse, own, other, half, width):
    panel, rank = own.shape
    whole = pl.BlockSpec(memory_space=pltpu.VMEM)
    return pl.pallas_call(
        basis_kernel,
        grid_spec=pltpu.PrefetchScalarGridSpec(
            num_scalar_prefetch=1,
            grid=(),
            in_specs=[whole] * 3,
            out_specs=[whole] * 3,
            scratch_shapes=[pltpu.VMEM((half, rank), jnp.float32)],
        ),
        out_shape=[
            jax.ShapeDtypeStruct((half, 2 * panel), jnp.bfloat16),
            jax.ShapeDtypeStruct((half, 2 * panel), jnp.bfloat16),
            jax.ShapeDtypeStruct((panel, width), jnp.bfloat16),
        ],
        compiler_params=pltpu.CompilerParams(vmem_limit_bytes=32 * MIB),
        cost_estimate=pl.CostEstimate(
            flops=12 * rank * panel * (2 * half + width), bytes_accessed=6 * rank * panel, transcendentals=0
        ),
        name="basis_parts",
    )(at, inverse, own, other)


def product_kernel(scale, left_ref, own_ref, other_ref, *out_refs):
    rows = own_ref.shape[0]
    total = jnp.dot(left_ref[:, :rows], own_ref[...], preferred_element_type=jnp.float32)
    total += jnp.dot(left_ref[:, rows:], other_ref[...], preferred_element_type=jnp.float32)
    total *= scale
    start = 0
    for out_ref in out_refs:
        end = start + out_ref.shape[0]
        out_ref[...] = total[start:end].astype(out_ref.dtype)
        start = end


def product(left, own, other, first, width, steps, scale):
    rows = own.shape[0]
    half = left.shape[0]
    count = width * steps
    size = half // len(PIECES)
    heights = [size * len(g) for g in (FORWARD, BACKWARD, STAY)]
    spec = pl.BlockSpec(
        (pl.Element(rows), pl.Element(width)), lambda k: (0, pl.multiple_of(first + k * width, BLK))
    )
    return pl.pallas_call(
        functools.partial(product_kernel, scale),
        grid=(steps,),
        in_specs=[pl.BlockSpec((half, 2 * rows), lambda k: (0, 0)), spec, spec],
        out_specs=[pl.BlockSpec((height, width), lambda k: (0, k)) for height in heights],
        out_shape=[
            jax.ShapeDtypeStruct((height, count), jnp.float32 if i == 2 else jnp.bfloat16)
            for i, height in enumerate(heights)
        ],
        compiler_params=pltpu.CompilerParams(vmem_limit_bytes=40 * MIB),
        cost_estimate=pl.CostEstimate(
            flops=4 * half * rows * count,
            bytes_accessed=(4 * rows + 2 * half) * count,
            transcendentals=0,
        ),
        name="product",
    )(left, own, other)


def on_device(blocks, owner, block_pos, omega):
    slot_count = blocks.shape[0]
    rank = omega.shape[1]
    chips = lax.axis_size("chips")
    row_devices = 2 * chips
    col_devices = lax.axis_size("cols")
    devices_all = row_devices * col_devices
    everywhere = ("chips", "core", "cols")
    capacity = max(2, 2 * slot_count // devices_all)
    slots = devices_all * capacity
    panel, cols = PBR * BLK, TBC * BLK
    total_rows = panel * row_devices
    core = lax.axis_index("core")
    swap = functools.partial(lax.ppermute, axis_name="core", perm=[(0, 1), (1, 0)])

    target = owner[:, 0]
    numbers = jnp.arange(slot_count, dtype=jnp.int32)
    same = (target[:, None] == target[None, :]) & (numbers[None, :] < numbers[:, None])
    place = target * capacity + jnp.sum(same.astype(jnp.int32), axis=1)
    spots = jnp.arange(slots, dtype=jnp.int32)
    hit = place[None, :] == spots[:, None]
    send_where = jnp.sum(jnp.where(hit, block_pos[None, :] + 1, 0), axis=1)
    send_blocks = bucket(place, blocks, slots)
    got_blocks = lax.all_to_all(
        send_blocks.reshape(devices_all, capacity, BLK, BLK), everywhere, 0, 0, tiled=True
    ).reshape(slots, BLK, BLK)
    got_where = lax.all_to_all(
        send_where.reshape(devices_all, capacity), everywhere, 0, 0, tiled=True
    ).reshape(slots)

    key = jnp.where(got_where == 0, PBR * TBC, got_where - 1)
    before = (key[None, :] < key[:, None]) | (
        (key[None, :] == key[:, None]) & (spots[None, :] < spots[:, None])
    )
    order = jnp.sum(before.astype(jnp.int32), axis=1)
    packed = key * slots + spots
    ordered = jnp.sum(jnp.where(order[None, :] == spots[:, None], packed[None, :], 0), axis=1)
    slot, where = ordered % slots, ordered // slots
    again = jnp.concatenate([jnp.zeros((1,), jnp.int32), (where[1:] == where[:-1]).astype(jnp.int32)])
    later = jnp.concatenate([jnp.zeros((1,), jnp.int32), again[:-1]])
    code = slot + (where // TBC) * 256 + (where % TBC) * 1024 + (again << 17) + (later << 18)
    filled = jnp.sum((key < PBR * TBC).astype(jnp.int32))
    code = jnp.concatenate([code, filled[None]])

    tile, part = tile_and_sketch(code, got_blocks, omega, panel, cols)
    other_tile = swap(tile)

    share = panel // col_devices
    parts = lax.all_to_all(part.reshape(col_devices, share, rank), "cols", 0, 0, tiled=True)
    which = core.astype(jnp.int32)[None]
    own_share, keep, send = share_and_gram(which, parts)
    same_core = ("chips", "cols")
    gram_rows = (chips * col_devices, BLK // devices_all, keep.shape[1])
    grams = lax.all_to_all((keep + swap(send)).reshape(gram_rows), same_core, 0, 0, tiled=True)
    gram, late_share = lax.optimization_barrier(
        (jnp.broadcast_to(jnp.sum(grams, axis=0)[None], gram_rows), own_share)
    )
    gram = lax.all_to_all(gram, same_core, 0, 0, tiled=True).reshape(keep.shape)
    other_gram = swap(gram)
    shares = [late_share] + [
        lax.ppermute(late_share, "cols", [(i, (i + d) % col_devices) for i in range(col_devices)])
        for d in range(1, col_devices)
    ]
    back = jnp.stack(shares[::-1] * 2)
    start = col_devices - 1 - lax.axis_index("cols")
    sketch = lax.dynamic_slice_in_dim(back, start, col_devices, 0).reshape(panel, rank)
    other_sketch = swap(sketch)
    inverse = inverse_factor(which, gram, other_gram, rank, 1.0 / total_rows)

    ranks = rank // row_devices
    along = math.isqrt(chips)
    chip = lax.axis_index("chips")
    x, y = chip // along, chip % along
    at = [(((x + a) % along * along + (y + b) % along) * 2 + core) * ranks for a, b in PIECES]
    width = rank // col_devices
    at.append(lax.axis_index("cols") * width)
    left, turned, basis = basis_parts(
        jnp.stack(at).astype(jnp.int32), inverse, sketch, other_sketch, rank // 2, width
    )

    def shift(over_x, steps):
        moves = []
        for i in range(chips):
            a, b = divmod(i, along)
            a, b = ((a + steps) % along, b) if over_x else (a, (b + steps) % along)
            moves.append((i, a * along + b))
        return functools.partial(lax.ppermute, axis_name="chips", perm=moves)

    def multiply(first, count, factor):
        return product(factor, tile, other_tile, first, count // 2, 2, 1.0 / math.sqrt(total_rows))

    def scatter(ahead, behind, total, x_first):
        forward, backward = shift(x_first, 1), shift(x_first, -1)
        ahead, behind = forward(ahead), backward(behind)
        far, back_far = forward(ahead[: FAR * ranks]), backward(behind[: FAR * ranks])
        total += ahead[FAR * ranks :].astype(jnp.float32) + behind[FAR * ranks :].astype(jnp.float32)
        total += jnp.concatenate([far, back_far], axis=0).astype(jnp.float32)
        terms = [total[i * ranks : (i + 1) * ranks] for i in range(along)]
        result = terms[0]
        for i in range(1, along):
            result += shift(not x_first, i)(terms[i].astype(jnp.bfloat16)).astype(jnp.float32)
        return result

    quarter = cols // 4
    coefficients = jnp.concatenate(
        [
            scatter(*multiply(i * quarter, quarter, (left, turned)[i % 2]), i % 2 == 0)
            for i in range(4)
        ],
        axis=1,
    )
    return basis, coefficients


def solution(mesh):
    rows, cols = mesh.devices.shape
    mesh = jax.sharding.Mesh(mesh.devices.reshape(rows // 2, 2, cols), ("chips", "core", "cols"))
    everywhere = ("chips", "core", "cols")
    in_specs = (P(everywhere, None, None), P(everywhere, None), P(everywhere), P("cols", None))
    out_specs = (P(("chips", "core"), "cols"), P(("chips", "core"), "cols"))
    return jax.shard_map(
        on_device, mesh=mesh, in_specs=in_specs, out_specs=out_specs, check_vma=False
    )
```

```python
import functools
import math

import jax
import jax.numpy as jnp
from jax import lax
from jax.experimental import pallas as pl
from jax.experimental.pallas import tpu as pltpu
from jax.sharding import PartitionSpec as P

PBR = 4
TBC = 104
BLK = 128
HIGHEST = lax.Precision.HIGHEST
MIB = 1 << 20


def bucket_kernel(place_ref, blocks_ref, out_ref, sem):
    count = blocks_ref.shape[0]

    def issue(slot, carry):
        pltpu.make_async_copy(blocks_ref.at[slot], out_ref.at[place_ref[slot]], sem).start()
        return carry

    lax.fori_loop(0, count, issue, 0)
    pltpu.make_async_copy(blocks_ref, out_ref.at[pl.ds(0, count)], sem).wait()


def bucket(place, blocks, slots):
    return pl.pallas_call(
        bucket_kernel,
        grid_spec=pltpu.PrefetchScalarGridSpec(
            num_scalar_prefetch=1,
            grid=(),
            in_specs=[pl.BlockSpec(memory_space=pltpu.VMEM)],
            out_specs=pl.BlockSpec(memory_space=pl.ANY),
            scratch_shapes=[pltpu.SemaphoreType.DMA],
        ),
        out_shape=jax.ShapeDtypeStruct((slots,) + blocks.shape[1:], blocks.dtype),
        compiler_params=pltpu.CompilerParams(vmem_limit_bytes=56 * MIB),
        cost_estimate=pl.CostEstimate(flops=0, bytes_accessed=2 * blocks.size * 2, transcendentals=0),
        name="bucket",
    )(place, blocks)


def tile_kernel(code_ref, got_hbm, omega_hbm, tile_hbm, sketch_ref, got, omega, tile, total, sems):
    slots = got.shape[0]
    rows, cols = tile.shape
    get_blocks = pltpu.make_async_copy(got_hbm, got, sems.at[0])
    get_omega = pltpu.make_async_copy(omega_hbm, omega, sems.at[1])
    get_blocks.start()
    get_omega.start()

    def clear(step, carry):
        tile[pl.ds(pl.multiple_of(step * 16, 16), 16), :] = jnp.zeros((16, cols), tile.dtype)
        return carry

    lax.fori_loop(0, rows // 16, clear, 0)
    get_blocks.wait()

    def insert(step, carry):
        code = code_ref[step]
        slot = code & 255
        row = pl.multiple_of(((code >> 8) & 3) * BLK, BLK)
        col = pl.multiple_of(((code >> 10) & 127) * BLK, BLK)
        again = (code >> 17) & 1
        later = (code >> 18) & 1

        @pl.when(again == 0)
        def _():
            tile[pl.ds(row, BLK), pl.ds(col, BLK)] = got[slot]

        @pl.when(again == 1)
        def _():
            @pl.when(later == 0)
            def _():
                total[...] = got[code_ref[step - 1] & 255].astype(jnp.float32)

            value = total[...] + got[slot].astype(jnp.float32)
            total[...] = value
            tile[pl.ds(row, BLK), pl.ds(col, BLK)] = value.astype(tile.dtype)

        return carry

    lax.fori_loop(0, code_ref[slots], insert, 0)
    put_tile = pltpu.make_async_copy(tile, tile_hbm, sems.at[2])
    put_tile.start()
    get_omega.wait()
    sketch_ref[...] = jnp.zeros_like(sketch_ref)
    depth = 1024

    def multiply(step, carry):
        at = pl.ds(pl.multiple_of(step * depth, depth), depth)
        sketch_ref[...] += jnp.dot(tile[:, at], omega[at, :], preferred_element_type=jnp.float32)
        return carry

    lax.fori_loop(0, cols // depth, multiply, 0)
    put_tile.wait()


def tile_and_sketch(code, got, omega, rows, cols):
    slots, rank = got.shape[0], omega.shape[1]
    return pl.pallas_call(
        tile_kernel,
        grid_spec=pltpu.PrefetchScalarGridSpec(
            num_scalar_prefetch=1,
            grid=(),
            in_specs=[pl.BlockSpec(memory_space=pl.ANY)] * 2,
            out_specs=[
                pl.BlockSpec(memory_space=pl.ANY),
                pl.BlockSpec(memory_space=pltpu.VMEM),
            ],
            scratch_shapes=[
                pltpu.VMEM((slots, BLK, BLK), jnp.bfloat16),
                pltpu.VMEM((cols, rank), jnp.bfloat16),
                pltpu.VMEM((rows, cols), jnp.bfloat16),
                pltpu.VMEM((BLK, BLK), jnp.float32),
                pltpu.SemaphoreType.DMA((3,)),
            ],
        ),
        out_shape=[
            jax.ShapeDtypeStruct((rows, cols), jnp.bfloat16),
            jax.ShapeDtypeStruct((rows, rank), jnp.float32),
        ],
        compiler_params=pltpu.CompilerParams(vmem_limit_bytes=52 * MIB),
        cost_estimate=pl.CostEstimate(
            flops=2 * rows * cols * rank,
            bytes_accessed=2 * (got.size + omega.size + rows * cols),
            transcendentals=0,
        ),
        name="tile_and_sketch",
    )(code, got, omega)


def upper_rows(n):
    start = 0
    for at in range(0, n, BLK):
        yield at, start, n - at
        start += n - at


def gram_kernel(core_ref, parts_ref, share_ref, keep_ref, send_ref, packed):
    share = parts_ref[0]
    for i in range(1, parts_ref.shape[0]):
        share += parts_ref[i]
    share_ref[...] = share
    for at, start, width in upper_rows(share.shape[1]):
        packed[:, start : start + width] = lax.dot_general(
            share[:, at : at + BLK],
            share[:, at:],
            (((0,), (0,)), ((), ())),
            precision=HIGHEST,
            preferred_element_type=jnp.float32,
        )
    half = keep_ref.shape[0]
    keep_ref[...] = packed[pl.ds(pl.multiple_of(core_ref[0] * half, half), half), :]
    send_ref[...] = packed[pl.ds(pl.multiple_of((1 - core_ref[0]) * half, half), half), :]


def share_and_gram(core, parts):
    _, share, rank = parts.shape
    packed = sum(width for _, _, width in upper_rows(rank))
    whole = pl.BlockSpec(memory_space=pltpu.VMEM)
    return pl.pallas_call(
        gram_kernel,
        grid_spec=pltpu.PrefetchScalarGridSpec(
            num_scalar_prefetch=1,
            grid=(),
            in_specs=[whole],
            out_specs=[whole] * 3,
            scratch_shapes=[pltpu.VMEM((BLK, packed), jnp.float32)],
        ),
        out_shape=[
            jax.ShapeDtypeStruct((share, rank), jnp.float32),
            jax.ShapeDtypeStruct((BLK // 2, packed), jnp.float32),
            jax.ShapeDtypeStruct((BLK // 2, packed), jnp.float32),
        ],
        compiler_params=pltpu.CompilerParams(vmem_limit_bytes=24 * MIB),
        cost_estimate=pl.CostEstimate(
            flops=12 * share * rank * rank, bytes_accessed=8 * parts.size, transcendentals=0
        ),
        name="share_and_gram",
    )(core, parts)


def factor_kernel(scale, core_ref, mine_ref, other_ref, out_ref, work):
    n = work.shape[0]
    work[...] = jnp.zeros_like(work)
    for at, start, width in upper_rows(n):
        for core, rows_ref in ((core_ref[0], mine_ref), (1 - core_ref[0], other_ref)):
            half = rows_ref.shape[0]
            rows = pl.ds(pl.multiple_of(at + core * half, half), half)
            work[rows, at:] = rows_ref[:, start : start + width] * scale
    row = lax.broadcasted_iota(jnp.int32, (n, n), 0)
    lane = lax.broadcasted_iota(jnp.int32, (n, n), 1)
    out_ref[...] = jnp.where(row == lane, 1.0, 0.0)
    sub = lax.broadcasted_iota(jnp.int32, (8, BLK), 0)
    lane8 = lax.broadcasted_iota(jnp.int32, (8, BLK), 1)
    groups = BLK // 8

    def spread(value, j):
        return jnp.broadcast_to(value[:, j : j + 1], (8, BLK))

    def block(panel, carry):
        at = pl.ds(pl.multiple_of(panel * BLK, BLK), BLK)
        left = [work[pl.ds(pl.multiple_of(panel * BLK + 8 * g, 8), 8), at] for g in range(groups)]
        right = [jnp.where(lane8 == sub + 8 * g, 1.0, 0.0) for g in range(groups)]
        for g0 in range(groups):
            own = [spread(left[g0], 8 * g0 + k) for k in range(8)]
            factors, pivots_left, pivots_right = {}, [], []
            for k in range(8):
                inverse = 1.0 / own[k][k : k + 1, :]
                for later in range(k + 1, 8):
                    factors[k, later] = own[later][k : k + 1, :] * inverse
                    own[later] = own[later] - own[k] * factors[k, later]
                pivots_left.append(left[g0][k : k + 1, :] * inverse)
                pivots_right.append(right[g0][k : k + 1, :] * inverse)
                column = jnp.where(sub > k, own[k], 0.0)
                left[g0] = left[g0] - column * pivots_left[k]
                right[g0] = right[g0] - column * pivots_right[k]
            for g in range(g0 + 1, groups):
                below = [spread(left[g], 8 * g0 + k) for k in range(8)]
                for k in range(8):
                    for later in range(k + 1, 8):
                        below[later] = below[later] - below[k] * factors[k, later]
                    left[g] = left[g] - below[k] * pivots_left[k]
                    right[g] = right[g] - below[k] * pivots_right[k]
        halves = []
        for g in range(groups):
            pivot = jnp.sum(
                jnp.where(lane8 == sub + 8 * g, left[g], 0.0), axis=1, keepdims=True
            )
            halves.append(right[g] * (1.0 / jnp.sqrt(pivot)))
        inverse_block = jnp.concatenate(halves, axis=0)
        both = jnp.concatenate([work[at, :], out_ref[at, :]], axis=1)
        upper = jnp.dot(inverse_block, both, precision=HIGHEST, preferred_element_type=jnp.float32)

        @pl.when(panel < n // BLK - 1)
        def _():
            lanes = lax.broadcasted_iota(jnp.int32, (BLK, n), 1)
            later = jnp.where(lanes >= (panel + 1) * BLK, upper[:, :n], 0.0)
            change = lax.dot_general(
                later, upper, (((0,), (0,)), ((), ())), precision=HIGHEST, preferred_element_type=jnp.float32
            )
            work[...] -= change[:, :n]
            out_ref[...] -= change[:, n:]

        out_ref[at, :] = upper[:, n:]
        return carry

    lax.fori_loop(0, n // BLK, block, 0)


def inverse_factor(core, mine, other, n, scale):
    whole = pl.BlockSpec(memory_space=pltpu.VMEM)
    return pl.pallas_call(
        functools.partial(factor_kernel, scale),
        grid_spec=pltpu.PrefetchScalarGridSpec(
            num_scalar_prefetch=1,
            grid=(),
            in_specs=[whole] * 2,
            out_specs=whole,
            scratch_shapes=[pltpu.VMEM((n, n), jnp.float32)],
        ),
        out_shape=jax.ShapeDtypeStruct((n, n), jnp.float32),
        compiler_params=pltpu.CompilerParams(vmem_limit_bytes=24 * MIB),
        cost_estimate=pl.CostEstimate(
            flops=1 << 35, bytes_accessed=2 * n * n * 4, transcendentals=0
        ),
        name="inverse_factor",
    )(core, mine, other)


FAR = 2
FORWARD = ((2, 0), (2, 1)) + tuple((1, e) for e in range(4))
BACKWARD = ((2, 2), (2, 3)) + tuple((3, e) for e in range(4))
STAY = tuple((0, e) for e in range(4))
PIECES = FORWARD + BACKWARD + STAY


def basis_kernel(at_ref, inverse_ref, own_ref, other_ref, left_ref, turned_ref, basis_ref, chosen):
    pieces = len(PIECES)
    size = chosen.shape[0] // pieces
    panel = own_ref.shape[0]
    for k in range(pieces):
        chosen[k * size : (k + 1) * size, :] = inverse_ref[
            pl.ds(pl.multiple_of(at_ref[k], size), size), :
        ]
    contract = (((1,), (1,)), ((), ()))
    for i, sketch_ref in enumerate((own_ref, other_ref)):
        left = lax.dot_general(
            chosen[...], sketch_ref[...], contract, precision=HIGHEST, preferred_element_type=jnp.float32
        ).astype(left_ref.dtype)
        left_ref[:, i * panel : (i + 1) * panel] = left
        turned_ref[:, i * panel : (i + 1) * panel] = jnp.concatenate(
            [left[PIECES.index((b, a)) * size :][:size] for a, b in PIECES], axis=0
        )
    width = basis_ref.shape[1]
    basis_ref[...] = lax.dot_general(
        own_ref[...],
        inverse_ref[pl.ds(pl.multiple_of(at_ref[pieces], width), width), :],
        contract,
        precision=HIGHEST,
        preferred_element_type=jnp.float32,
    ).astype(basis_ref.dtype)


def basis_parts(at, inverse, own, other, half, width):
    panel, rank = own.shape
    whole = pl.BlockSpec(memory_space=pltpu.VMEM)
    return pl.pallas_call(
        basis_kernel,
        grid_spec=pltpu.PrefetchScalarGridSpec(
            num_scalar_prefetch=1,
            grid=(),
            in_specs=[whole] * 3,
            out_specs=[whole] * 3,
            scratch_shapes=[pltpu.VMEM((half, rank), jnp.float32)],
        ),
        out_shape=[
            jax.ShapeDtypeStruct((half, 2 * panel), jnp.bfloat16),
            jax.ShapeDtypeStruct((half, 2 * panel), jnp.bfloat16),
            jax.ShapeDtypeStruct((panel, width), jnp.bfloat16),
        ],
        compiler_params=pltpu.CompilerParams(vmem_limit_bytes=32 * MIB),
        cost_estimate=pl.CostEstimate(
            flops=12 * rank * panel * (2 * half + width), bytes_accessed=6 * rank * panel, transcendentals=0
        ),
        name="basis_parts",
    )(at, inverse, own, other)


def product_kernel(scale, left_ref, own_ref, other_ref, *out_refs):
    rows = own_ref.shape[0]
    total = jnp.dot(left_ref[:, :rows], own_ref[...], preferred_element_type=jnp.float32)
    total += jnp.dot(left_ref[:, rows:], other_ref[...], preferred_element_type=jnp.float32)
    total *= scale
    start = 0
    for out_ref in out_refs:
        end = start + out_ref.shape[0]
        out_ref[...] = total[start:end].astype(out_ref.dtype)
        start = end


def product(left, own, other, first, width, steps, scale):
    rows = own.shape[0]
    half = left.shape[0]
    count = width * steps
    size = half // len(PIECES)
    heights = [size * len(g) for g in (FORWARD, BACKWARD, STAY)]
    spec = pl.BlockSpec(
        (pl.Element(rows), pl.Element(width)), lambda k: (0, pl.multiple_of(first + k * width, BLK))
    )
    return pl.pallas_call(
        functools.partial(product_kernel, scale),
        grid=(steps,),
        in_specs=[pl.BlockSpec((half, 2 * rows), lambda k: (0, 0)), spec, spec],
        out_specs=[pl.BlockSpec((height, width), lambda k: (0, k)) for height in heights],
        out_shape=[
            jax.ShapeDtypeStruct((height, count), jnp.float32 if i == 2 else jnp.bfloat16)
            for i, height in enumerate(heights)
        ],
        compiler_params=pltpu.CompilerParams(vmem_limit_bytes=40 * MIB),
        cost_estimate=pl.CostEstimate(
            flops=4 * half * rows * count,
            bytes_accessed=(4 * rows + 2 * half) * count,
            transcendentals=0,
        ),
        name="product",
    )(left, own, other)


def on_device(blocks, owner, block_pos, omega):
    slot_count = blocks.shape[0]
    rank = omega.shape[1]
    chips = lax.axis_size("chips")
    row_devices = 2 * chips
    col_devices = lax.axis_size("cols")
    devices_all = row_devices * col_devices
    everywhere = ("chips", "core", "cols")
    capacity = max(2, 2 * slot_count // devices_all)
    slots = devices_all * capacity
    panel, cols = PBR * BLK, TBC * BLK
    total_rows = panel * row_devices
    core = lax.axis_index("core")
    swap = functools.partial(lax.ppermute, axis_name="core", perm=[(0, 1), (1, 0)])

    target = owner[:, 0]
    numbers = jnp.arange(slot_count, dtype=jnp.int32)
    same = (target[:, None] == target[None, :]) & (numbers[None, :] < numbers[:, None])
    place = target * capacity + jnp.sum(same.astype(jnp.int32), axis=1)
    spots = jnp.arange(slots, dtype=jnp.int32)
    hit = place[None, :] == spots[:, None]
    send_where = jnp.sum(jnp.where(hit, block_pos[None, :] + 1, 0), axis=1)
    send_blocks = bucket(place, blocks, slots)
    got_blocks = lax.all_to_all(
        send_blocks.reshape(devices_all, capacity, BLK, BLK), everywhere, 0, 0, tiled=True
    ).reshape(slots, BLK, BLK)
    got_where = lax.all_to_all(
        send_where.reshape(devices_all, capacity), everywhere, 0, 0, tiled=True
    ).reshape(slots)

    key = jnp.where(got_where == 0, PBR * TBC, got_where - 1)
    before = (key[None, :] < key[:, None]) | (
        (key[None, :] == key[:, None]) & (spots[None, :] < spots[:, None])
    )
    order = jnp.sum(before.astype(jnp.int32), axis=1)
    packed = key * slots + spots
    ordered = jnp.sum(jnp.where(order[None, :] == spots[:, None], packed[None, :], 0), axis=1)
    slot, where = ordered % slots, ordered // slots
    again = jnp.concatenate([jnp.zeros((1,), jnp.int32), (where[1:] == where[:-1]).astype(jnp.int32)])
    later = jnp.concatenate([jnp.zeros((1,), jnp.int32), again[:-1]])
    code = slot + (where // TBC) * 256 + (where % TBC) * 1024 + (again << 17) + (later << 18)
    filled = jnp.sum((key < PBR * TBC).astype(jnp.int32))
    code = jnp.concatenate([code, filled[None]])

    tile, part = tile_and_sketch(code, got_blocks, omega, panel, cols)
    other_tile = swap(tile)

    share = panel // col_devices
    parts = lax.all_to_all(part.reshape(col_devices, share, rank), "cols", 0, 0, tiled=True)
    which = core.astype(jnp.int32)[None]
    own_share, keep, send = share_and_gram(which, parts)
    same_core = ("chips", "cols")
    gram_rows = (chips * col_devices, BLK // devices_all, keep.shape[1])
    grams = lax.all_to_all((keep + swap(send)).reshape(gram_rows), same_core, 0, 0, tiled=True)
    gram, late_share = lax.optimization_barrier(
        (jnp.broadcast_to(jnp.sum(grams, axis=0)[None], gram_rows), own_share)
    )
    gram = lax.all_to_all(gram, same_core, 0, 0, tiled=True).reshape(keep.shape)
    other_gram = swap(gram)
    shares = [late_share] + [
        lax.ppermute(late_share, "cols", [(i, (i + d) % col_devices) for i in range(col_devices)])
        for d in range(1, col_devices)
    ]
    back = jnp.stack(shares[::-1] * 2)
    start = col_devices - 1 - lax.axis_index("cols")
    sketch = lax.dynamic_slice_in_dim(back, start, col_devices, 0).reshape(panel, rank)
    other_sketch = swap(sketch)
    inverse = inverse_factor(which, gram, other_gram, rank, 1.0 / total_rows)

    ranks = rank // row_devices
    along = math.isqrt(chips)
    chip = lax.axis_index("chips")
    x, y = chip // along, chip % along
    at = [(((x + a) % along * along + (y + b) % along) * 2 + core) * ranks for a, b in PIECES]
    width = rank // col_devices
    at.append(lax.axis_index("cols") * width)
    left, turned, basis = basis_parts(
        jnp.stack(at).astype(jnp.int32), inverse, sketch, other_sketch, rank // 2, width
    )

    def shift(over_x, steps):
        moves = []
        for i in range(chips):
            a, b = divmod(i, along)
            a, b = ((a + steps) % along, b) if over_x else (a, (b + steps) % along)
            moves.append((i, a * along + b))
        return functools.partial(lax.ppermute, axis_name="chips", perm=moves)

    def multiply(first, count, factor):
        return product(factor, tile, other_tile, first, count // 2, 2, 1.0 / math.sqrt(total_rows))

    def first_axis(ahead, behind, total, x_first):
        forward, backward = shift(x_first, 1), shift(x_first, -1)
        ahead, behind = forward(ahead), backward(behind)
        far, back_far = forward(ahead[: FAR * ranks]), backward(behind[: FAR * ranks])
        total += ahead[FAR * ranks :].astype(jnp.float32) + behind[FAR * ranks :].astype(jnp.float32)
        total += jnp.concatenate([far, back_far], axis=0).astype(jnp.float32)
        return total

    def second_axis(totals, x_first):
        total = jnp.concatenate(totals, axis=1)
        terms = [total[i * ranks : (i + 1) * ranks] for i in range(along)]
        result = terms[0]
        for i in range(1, along):
            result += shift(not x_first, i)(terms[i].astype(jnp.bfloat16)).astype(jnp.float32)
        return result

    quarter = cols // 4
    totals = [None] * 4
    for i in (0, 2, 1, 3):
        x_first = i < 2
        parts = multiply(i * quarter, quarter, left if x_first else turned)
        totals[i] = first_axis(*parts, x_first)
    coefficients = jnp.concatenate(
        [second_axis(totals[:2], True), second_axis(totals[2:], False)], axis=1
    )
    return basis, coefficients


def solution(mesh):
    rows, cols = mesh.devices.shape
    mesh = jax.sharding.Mesh(mesh.devices.reshape(rows // 2, 2, cols), ("chips", "core", "cols"))
    everywhere = ("chips", "core", "cols")
    in_specs = (P(everywhere, None, None), P(everywhere, None), P(everywhere), P("cols", None))
    out_specs = (P(("chips", "core"), "cols"), P(("chips", "core"), "cols"))
    return jax.shard_map(
        on_device, mesh=mesh, in_specs=in_specs, out_specs=out_specs, check_vma=False
    )
```
